32 devices in a mesh: expert: 16 (over z, y, x), tensor: 2 (over core).
Axes of the slice: x: 2, y: 2, z: 4, core: 2. Of those that a mesh axis runs over, the one named last changes fastest.
Arguments:
- tokens: bfloat16 [2048, 3584], P('expert'), may hold values from -6 to 6
- grad_out: bfloat16 [2048, 3584], P('expert'), may hold values from -6 to 6
- routes: int32 [2048, 2], P('expert'), may hold values from 0 to 15, all different within a row; in each aligned block of 128 rows (0 to 127, 128 to 255, ...) at most 48 rows name the same one
- probs: bfloat16 [2048, 2], P('expert'), may hold values from 0.049804688 to 0.5
- w_gate: bfloat16 [16, 3584, 1024], P('expert', None, 'tensor'), may hold values from -0.09375 to 0.09375
- w_up: bfloat16 [16, 3584, 1024], P('expert', None, 'tensor'), may hold values from -0.09375 to 0.09375
- w_down: bfloat16 [16, 1024, 3584], P('expert', 'tensor'), may hold values from -0.1875 to 0.1875
Outputs:
- d_tokens: bfloat16 [2048, 3584], P('expert')
- d_probs: bfloat16 [2048, 2], P('expert')
- d_gate: bfloat16 [16, 3584, 1024], P('expert', None, 'tensor')
- d_up: bfloat16 [16, 3584, 1024], P('expert', None, 'tensor')
- d_down: bfloat16 [16, 1024, 3584], P('expert', 'tensor')
The draws below stay inside these ranges and needn't reach their ends.
Inputs may be any that keep to these rules, and one draw needn't show every extreme that they name: `routes`: each token names 2 different experts; among the 128 tokens held by one device along `expert` (one block) no expert is named more than 48 times, a bound that some expert reaches in some such blocks.
All inputs are finite; a program needn't handle non-finite values.
Results may differ from the reference program's by a relative error of at most 0.012.
Values may be sent and summed in bfloat16 or wider, within the bound.
No kernel may reach another device: no remote copies, remote signals or barrier semaphores. Data moves between devices by JAX's collectives and lax.ppermute only.
A program may use at most 192 MiB of HBM per device.

```python
import math
import jax
import jax.numpy as jnp
import numpy as np
from jax import lax

D = 3584
FF = 1024
TOP_WIN = 2
TOK_DEV = 128
EXPERTS = 16
TOKENS = 2048
CAP = 48
N_EXPERT = 16


def block_scale(rng, shape, cuts, smallest, high):
    factor_of, own = 1.0, jax.random.fold_in(rng, 6)
    for position, blocks in cuts:
        heights = jnp.exp(jax.random.uniform(jax.random.fold_in(own, position), (blocks,), jnp.float32, smallest / len(cuts), high / len(cuts)))
        factor_of = factor_of * jnp.repeat(heights, shape[position] // blocks).reshape([-1 if axis == position else 1 for axis in range(len(shape))])
    return factor_of


def assign_block(key, own, number, rows, number_of, top, most, slope):
    ranking = jax.random.permutation(key, number_of)
    crowded, ordinary = load_shares(number_of, rows * top, most, slope, True), load_shares(number_of, rows * top, most, slope, False)
    places = jnp.arange(number_of)

    def named(sizes, offset_by):
        used = int((sizes > 0).sum())
        fixed = max(1, used // 4)
        passed = fixed + (places - fixed + offset_by * (used - fixed)) % max(1, number_of - fixed)
        return jnp.zeros((number_of,), jnp.int32).at[ranking[jnp.where(places < fixed, places, passed)]].set(jnp.asarray(sizes, jnp.int32))

    sizes = jnp.where(number % 4 == 0, named(crowded, number // 4), named(ordinary, number - number // 4 - 1))
    mixed = jax.random.permutation(jax.random.fold_in(own, 3), number_of)
    donor, taker = mixed[0:number_of // 2 * 2:2], mixed[1:number_of // 2 * 2:2]
    room = jnp.minimum(sizes[donor] - 1, most - sizes[taker]) // 2
    room = jnp.where((donor == ranking[0]) | (taker == ranking[0]) | (sizes[taker] == 0), 0, jnp.maximum(room, 0))
    passed = jax.random.randint(jax.random.fold_in(own, 4), (number_of // 2,), 0, 1 << 20) % (room + 1)
    sizes = sizes.at[donor].add(-passed).at[taker].add(passed)
    members = jnp.searchsorted(jnp.cumsum(sizes), jnp.arange(rows * top), side="right").astype(jnp.int32)
    table = members.reshape(top, rows).T
    table = table[jax.random.permutation(jax.random.fold_in(own, 1), rows)]
    offset_by = jax.random.randint(jax.random.fold_in(own, 2), (rows, 1), 0, top)
    return jnp.take_along_axis(table, (jnp.arange(top)[None, :] + offset_by) % top, axis=1)


def load_shares(amount, total, most, slope, full):
    portions = [(1 << 20) // math.isqrt(rank ** slope) + 1 for rank in range(1, amount + 1)]
    largest = most if full else min(most, max(-(-total // amount), total * portions[0] // sum(portions)))
    least = 1 if total - largest >= amount - 1 else 0
    holding, surplus = [largest] + [least] * (amount - 1), total - largest - least * (amount - 1)
    while surplus > 0:
        movable = [i for i in range(1, amount) if holding[i] < largest] or [i for i in range(1, amount) if holding[i] < most]
        pool, budget = sum([portions[i] for i in movable]), surplus
        for i in movable:
            addition = min(most - holding[i], max(1, budget * portions[i] // pool), surplus)
            holding[i] = holding[i] + addition
            surplus = surplus - addition
    return np.array(holding)


def gaussian(own_key, dims, scale, limit, pieces=(), kind=jnp.bfloat16):
    gain = block_scale(own_key, dims, pieces, -0.22, 0.18) if pieces else 1.0
    entries = jax.random.normal(own_key, dims, jnp.float32) * scale * gain
    return jnp.minimum(jnp.maximum(entries, -limit), limit).astype(kind)


def setup_inputs(seed: int = 0) -> dict:
    keys = jax.random.split(jax.random.key(seed), 8)
    tokens = gaussian(keys[0], (TOKENS, D), 1.0, 6.0, ((0, 16),))
    grad_out = gaussian(keys[1], (TOKENS, D), 1.0, 6.0, ((0, 16),))
    routes_keys = jax.random.split(jax.random.fold_in(keys[2], 1), TOKENS // TOK_DEV)
    routes_turns = jax.random.permutation(jax.random.fold_in(keys[2], 3), TOKENS // TOK_DEV)
    routes = jax.vmap(lambda own, number: assign_block(jax.random.fold_in(keys[2], 2), own, number, TOK_DEV, EXPERTS, TOP_WIN, CAP, 2))(routes_keys, routes_turns).reshape((TOKENS, TOP_WIN))
    probs = jnp.clip(0.049804688 + 0.4501953 * jax.random.uniform(keys[3], (TOKENS, TOP_WIN), jnp.float32) ** block_scale(keys[3], (TOKENS, TOP_WIN), ((0, 16),), -0.2, 0.2), 0.049804688, 0.5).astype(jnp.bfloat16)
    w_gate = gaussian(keys[4], (EXPERTS, D, FF), D ** -0.5, 0.09375, ((0, 16), (2, 2)))
    w_up = gaussian(keys[5], (EXPERTS, D, FF), D ** -0.5, 0.09375, ((0, 16), (2, 2)))
    w_down = gaussian(keys[6], (EXPERTS, FF, D), FF ** -0.5, 0.1875, ((0, 16), (1, 2)))
    return dict(tokens=tokens, grad_out=grad_out, routes=routes, probs=probs, w_gate=w_gate, w_up=w_up, w_down=w_down)


def reference(tokens, grad_out, routes, probs, w_gate, w_up, w_down):
    rows = N_EXPERT * CAP
    flat = routes.reshape(N_EXPERT, TOK_DEV * TOP_WIN)
    onehot = (flat[:, :, None] == jnp.arange(EXPERTS, dtype=jnp.int32)[None, None, :]).astype(jnp.int32)
    slot = jnp.sum((jnp.cumsum(onehot, axis=1) - 1) * onehot, axis=2).astype(jnp.int32)
    block = jnp.arange(N_EXPERT, dtype=jnp.int32)[:, None]
    target = (flat * rows + block * CAP + slot).reshape(-1).astype(jnp.int32)
    pairs = jnp.arange(TOKENS * TOP_WIN, dtype=jnp.int32)
    filled = jnp.zeros((EXPERTS * rows,), jnp.int32).at[target].set(pairs + 1)
    filled = filled.reshape(EXPERTS, rows)
    prob_flat = probs.reshape(-1).astype(jnp.float32)

    def one_expert(carry, items):
        d_tok, d_prob = carry
        ids, gate_w, up_w, down_w = items
        live = ids > 0
        pair = jnp.maximum(ids - 1, 0)
        owner = pair // TOP_WIN
        keep = live[:, None]
        xe = jnp.where(keep, tokens[owner], jnp.zeros((), jnp.bfloat16))
        dye = jnp.where(keep, grad_out[owner], jnp.zeros((), jnp.bfloat16))
        pe = jnp.where(live, prob_flat[pair], jnp.zeros((), jnp.float32))
        gate = jnp.dot(xe, gate_w, preferred_element_type=jnp.float32)
        up = jnp.dot(xe, up_w, preferred_element_type=jnp.float32)
        sg = jax.nn.sigmoid(gate)
        act = gate * sg
        hidden = (act * up).astype(jnp.bfloat16)
        raw = jnp.dot(dye, down_w.T, preferred_element_type=jnp.float32)
        row_dp = jnp.sum(hidden.astype(jnp.float32) * raw, axis=1)
        dh = pe[:, None] * raw
        g_up = (dh * act).astype(jnp.bfloat16)
        g_gate = (dh * up * sg * (1.0 + gate * (1.0 - sg))).astype(jnp.bfloat16)
        scaled = (pe[:, None] * dye.astype(jnp.float32)).astype(jnp.bfloat16)
        grad_gate = jnp.dot(xe.T, g_gate, preferred_element_type=jnp.float32).astype(jnp.bfloat16)
        grad_up = jnp.dot(xe.T, g_up, preferred_element_type=jnp.float32).astype(jnp.bfloat16)
        grad_down = jnp.dot(hidden.T, scaled, preferred_element_type=jnp.float32).astype(jnp.bfloat16)
        contrib = (jnp.dot(g_gate, gate_w.T, preferred_element_type=jnp.float32)
                   + jnp.dot(g_up, up_w.T, preferred_element_type=jnp.float32)).astype(jnp.bfloat16)
        d_tok = d_tok.at[owner].add(jnp.where(keep, contrib.astype(jnp.float32), jnp.zeros((), jnp.float32)))
        d_prob = d_prob.at[pair].add(jnp.where(live, row_dp, jnp.zeros((), jnp.float32)))
        return (d_tok, d_prob), (grad_gate, grad_up, grad_down)

    start = (jnp.zeros((TOKENS, D), jnp.float32), jnp.zeros((TOKENS * TOP_WIN,), jnp.float32))
    (d_tok, d_prob), (d_gate, d_up, d_down) = lax.scan(one_expert, start, (filled, w_gate, w_up, w_down))
    return (d_tok.astype(jnp.bfloat16), d_prob.reshape(TOKENS, TOP_WIN).astype(jnp.bfloat16), d_gate, d_up, d_down)
```

```python
import jax
import jax.numpy as jnp
from jax import lax
from jax.sharding import PartitionSpec as P

BF16 = jnp.bfloat16
F32 = jnp.float32
LANES = 128


def dot(a, b, dims):
    return lax.dot_general(a, b, (dims, ((), ())), preferred_element_type=F32)


def split_axis_sizes(experts):
    rings = 4 if experts % 4 == 0 else 1
    return rings, experts // rings


def slots_in_block(routes, experts):
    tok = routes.shape[0]
    ids = jnp.arange(experts, dtype=jnp.int32)[None, :]
    hot = [(routes[:, k : k + 1] == ids) for k in range(routes.shape[1])]
    named = sum(h.astype(F32) for h in hot).astype(BF16)
    before = (jnp.arange(tok)[:, None] > jnp.arange(tok)[None, :]).astype(BF16)
    counts = dot(before, named, ((1,), (0,)))
    return jnp.stack([jnp.sum(jnp.where(h, counts, 0.0), axis=1) for h in hot], axis=1)


def on_device(tokens, grad_out, routes, probs, w_gate, w_up, w_down):
    experts = lax.axis_size("expert")
    tok, width = tokens.shape
    top = routes.shape[1]
    cap = 3 * tok * top // experts
    rings, plane = split_axis_sizes(experts)
    half = width // 2
    me = lax.axis_index("expert")
    core = lax.axis_index("tensor")
    z, p = me // plane, me % plane
    gate_w, up_w, down_w = w_gate[0], w_up[0], w_down[0]

    ring = [(i, (i + plane) % experts) for i in range(experts)]
    peers = [[(i, i // plane * plane + ((i % plane) ^ j)) for i in range(experts)] for j in range(plane)]
    swap = [(0, 1), (1, 0)]

    slot = slots_in_block(routes, experts)
    aux = jnp.concatenate([routes.astype(BF16), slot.astype(BF16), probs], axis=1)
    aux = jnp.pad(aux, ((0, 0), (0, LANES - 3 * top)))
    x_half = lax.dynamic_slice_in_dim(tokens, core * half, half, axis=1)
    dy_half = lax.dynamic_slice_in_dim(grad_out, core * half, half, axis=1)
    block = jnp.concatenate([x_half, dy_half, aux], axis=1)

    row = jnp.arange(plane * cap, dtype=jnp.int32)
    code_of_row = (z * plane + (p ^ (row // cap))) * cap + row % cap

    def picks(block):
        aux = block[:, 2 * half :].astype(F32)
        out = []
        for k in range(top):
            code = (aux[:, k] * cap + aux[:, top + k]).astype(jnp.int32)
            out.append(code_of_row[:, None] == code[None, :])
        return out, aux[:, 2 * top : 3 * top]

    def exchange(rows):
        parts = [rows[:cap]]
        for j in range(1, plane):
            parts.append(lax.ppermute(rows[j * cap : (j + 1) * cap], "expert", peers[j]))
        return jnp.concatenate(parts, axis=0)

    def in_order(own, other):
        return jnp.where(core == 0, jnp.concatenate([own, other], axis=1), jnp.concatenate([other, own], axis=1))

    held = [block]
    for _ in range(rings - 1):
        held.append(lax.ppermute(held[-1], "expert", ring))

    xs, gs, us, hs, ss, sums = [], [], [], [], [], []
    for k in range(rings):
        hit, prob = picks(held[k])
        both = sum(h.astype(F32) for h in hit).astype(BF16)
        sent = dot(both, held[k][:, : 2 * half], ((1,), (0,))).astype(BF16)
        weight = sum(jnp.sum(jnp.where(hit[r], prob[:, r][None, :], 0.0), axis=1, keepdims=True) for r in range(top))
        sent = jnp.concatenate([sent, jnp.broadcast_to(weight, (plane * cap, LANES)).astype(BF16)], axis=1)
        got = exchange(sent)
        other = lax.ppermute(got[:, : 2 * half], "tensor", swap)
        rows_x = in_order(got[:, :half], other[:, :half])
        rows_dy = in_order(got[:, half : 2 * half], other[:, half:])
        rows_p = got[:, 2 * half : 2 * half + 1].astype(F32)

        gate = dot(rows_x, gate_w, ((1,), (0,)))
        up = dot(rows_x, up_w, ((1,), (0,)))
        sigma = jax.nn.sigmoid(gate)
        act = gate * sigma
        hidden = (act * up).astype(BF16)
        raw = dot(rows_dy, down_w, ((1,), (1,)))
        row_part = jnp.sum(hidden.astype(F32) * raw, axis=1, keepdims=True)
        grad_h = rows_p * raw
        g_up = (grad_h * act).astype(BF16)
        g_gate = (grad_h * up * sigma * (1.0 + gate * (1.0 - sigma))).astype(BF16)
        scaled = (rows_p * rows_dy.astype(F32)).astype(BF16)
        partial = dot(g_gate, gate_w, ((1,), (1,))) + dot(g_up, up_w, ((1,), (1,)))

        high = lax.reduce_precision(row_part, 8, 7)
        dp = jnp.concatenate([high, row_part - high], axis=1).astype(BF16)
        dp = jnp.pad(dp, ((0, 0), (0, LANES - 2)))
        mine = lax.dynamic_slice_in_dim(partial, core * half, half, axis=1)
        theirs = lax.dynamic_slice_in_dim(partial, (1 - core) * half, half, axis=1).astype(BF16)
        came = lax.ppermute(jnp.concatenate([theirs, dp], axis=1), "tensor", swap)
        total = (mine + came[:, :half].astype(F32)).astype(BF16)
        total_dp = dp.astype(F32) + came[:, half:].astype(F32)
        total_dp = jnp.broadcast_to(total_dp[:, 0:1] + total_dp[:, 1:2], (plane * cap, LANES)).astype(BF16)
        back = exchange(jnp.concatenate([total, total_dp], axis=1))
        tok_sum = dot(both, back[:, :half], ((0,), (0,)))
        tok_dp = [dot(h.astype(BF16), back[:, half:], ((0,), (0,))) for h in hit]
        lane = jnp.arange(LANES)[None, :]
        tok_dp = sum(jnp.where(lane == r, tok_dp[r], 0.0) for r in range(top))
        sums.append(jnp.concatenate([tok_sum, tok_dp], axis=1))
        xs.append(rows_x)
        gs.append(g_gate)
        us.append(g_up)
        hs.append(hidden)
        ss.append(scaled)

    total = sums[1 % rings].astype(BF16) if rings > 1 else None
    for k in range(2, rings + 1):
        total = lax.ppermute(total, "expert", ring)
        total = (total.astype(F32) + sums[k % rings]).astype(BF16)
    if rings == 1:
        total = sums[0].astype(BF16)
    partner = lax.ppermute(total, "tensor", swap)
    d_tokens = in_order(total[:, :half], partner[:, :half])
    d_probs = jnp.where(core == 0, total[:, half : half + top], partner[:, half : half + top])

    xs, gs, us, hs, ss = (jnp.concatenate(a, axis=0) for a in (xs, gs, us, hs, ss))
    d_gate = dot(xs, gs, ((0,), (0,))).astype(BF16)[None]
    d_up = dot(xs, us, ((0,), (0,))).astype(BF16)[None]
    d_down = dot(hs, ss, ((0,), (0,))).astype(BF16)[None]
    return (d_tokens, d_probs, d_gate, d_up, d_down)


def solution(mesh):
    rows = P("expert", None)
    columns = P("expert", None, "tensor")
    down = P("expert", "tensor", None)
    return jax.shard_map(
        on_device,
        mesh=mesh,
        in_specs=(rows, rows, rows, rows, columns, columns, down),
        out_specs=(rows, rows, columns, columns, down),
        check_vma=False,
    )
```

```python
import functools

import jax
import jax.numpy as jnp
from jax import lax
from jax.experimental import pallas as pl
from jax.experimental.pallas import tpu as pltpu
from jax.sharding import PartitionSpec as P

BF16 = jnp.bfloat16
F32 = jnp.float32
LANES = 128
RINGS = 4
VMEM = pl.BlockSpec(memory_space=pltpu.VMEM)
SMEM = pl.BlockSpec(memory_space=pltpu.SMEM)
ANY = pl.BlockSpec(memory_space=pl.ANY)


def dot(a, b, dims):
    return lax.dot_general(a, b, (dims, ((), ())), preferred_element_type=F32)


def params(mib):
    return pltpu.CompilerParams(vmem_limit_bytes=mib * 2**20)


def cost(flops, nbytes):
    return pl.CostEstimate(flops=flops, bytes_accessed=nbytes, transcendentals=0)


def block_kernel(experts, top, tok_ref, dy_ref, routes_ref, probs_ref, out_ref):
    tok, half = tok_ref.shape
    lane = lax.broadcasted_iota(jnp.int32, (tok, LANES), 1)
    row = lax.broadcasted_iota(jnp.int32, (tok, tok), 0)
    col = lax.broadcasted_iota(jnp.int32, (tok, tok), 1)
    hot = [lane == routes_ref[:, k : k + 1] for k in range(top)]
    named = sum(jnp.where(h, 1.0, 0.0) for h in hot).astype(BF16)
    before = jnp.where(row > col, 1.0, 0.0).astype(BF16)
    counts = dot(before, named, ((1,), (0,)))
    aux = jnp.zeros((tok, LANES), F32)
    for k in range(top):
        slot = jnp.sum(jnp.where(hot[k], counts, 0.0), axis=1, keepdims=True)
        aux = jnp.where(lane == k, routes_ref[:, k : k + 1].astype(F32), aux)
        aux = jnp.where(lane == top + k, slot, aux)
        aux = jnp.where(lane == 2 * top + k, probs_ref[:, k : k + 1].astype(F32), aux)
    out_ref[:, :half] = tok_ref[...]
    out_ref[:, half : 2 * half] = dy_ref[...]
    out_ref[:, 2 * half :] = aux.astype(BF16)


def make_block(core, tokens, grad_out, routes, probs, experts):
    tok, width = tokens.shape
    top = routes.shape[1]
    half = width // 2
    mine = pl.BlockSpec((tok, half), lambda i, c: (0, c[0]))
    whole = pl.BlockSpec((tok, top), lambda i, c: (0, 0))

    def kernel(core_ref, *refs):
        block_kernel(experts, top, *refs)

    return pl.pallas_call(
        kernel,
        out_shape=jax.ShapeDtypeStruct((tok, 2 * half + LANES), BF16),
        grid_spec=pltpu.PrefetchScalarGridSpec(
            num_scalar_prefetch=1,
            grid=(1,),
            in_specs=[mine, mine, whole, whole],
            out_specs=pl.BlockSpec((tok, 2 * half + LANES), lambda i, c: (0, 0)),
        ),
        compiler_params=params(16),
        cost_estimate=cost(2 * tok * tok * LANES, 8 * tok * half),
    )(core, tokens, grad_out, routes, probs)


def hits(top, cap, aux, codes):
    turned = aux.astype(F32).T
    return [codes == turned[k : k + 1] * cap + turned[top + k : top + k + 1] for k in range(top)], turned


def choose_kernel(top, cap, codes_ref, block_ref, *outs):
    tok, wide = block_ref.shape
    body = wide - LANES
    hit, turned = hits(top, cap, block_ref[:, body:], codes_ref[:, :1])
    both = sum(jnp.where(h, 1.0, 0.0) for h in hit).astype(BF16)
    rows = dot(both, block_ref[:, :body], ((1,), (0,))).astype(BF16)
    prob = sum(jnp.where(hit[k], turned[2 * top + k : 2 * top + k + 1], 0.0) for k in range(top))
    prob = jnp.broadcast_to(jnp.sum(prob, axis=1, keepdims=True), (rows.shape[0], LANES)).astype(BF16)
    for j, out in enumerate(outs):
        out[:, :body] = rows[j * cap : (j + 1) * cap]
        out[:, body:] = prob[j * cap : (j + 1) * cap]


def choose(codes, block, top, cap):
    rows, wide = codes.shape[0], block.shape[1]
    return pl.pallas_call(
        functools.partial(choose_kernel, top, cap),
        out_shape=[jax.ShapeDtypeStruct((cap, wide), BF16)] * (rows // cap),
        in_specs=[VMEM, VMEM],
        out_specs=[VMEM] * (rows // cap),
        compiler_params=params(24),
        cost_estimate=cost(2 * rows * block.shape[0] * wide, 2 * wide * (rows + block.shape[0])),
    )(codes, block)


def expert_kernel(step, core_ref, own_ref, other_ref, wg_hbm, wu_hbm, wd_hbm, mine_ref, send_ref, ph_ref, gg_ref, gu_ref, wg, wu, wd, sems):
    half = own_ref.shape[1] // 2 // LANES * LANES
    parts = half // step
    copies = []
    for i in range(2 * parts):
        base = core_ref[0] if i < parts else 1 - core_ref[0]
        start = pl.multiple_of(base * half + i % parts * step, LANES)
        here = pl.ds(i * step, step)
        there = pl.ds(start, step)
        copies.append(
            [
                pltpu.make_async_copy(wg_hbm.at[there, :], wg.at[here, :], sems.at[0, i]),
                pltpu.make_async_copy(wu_hbm.at[there, :], wu.at[here, :], sems.at[1, i]),
                pltpu.make_async_copy(wd_hbm.at[:, there], wd.at[:, here], sems.at[2, i]),
            ]
        )
    for group in copies:
        for copy in group:
            copy.start()
    gate = up = raw = None
    for i in range(2 * parts):
        ref = own_ref if i < parts else other_ref
        at = i % parts * step
        x = ref[:, at : at + step]
        dy = ref[:, half + at : half + at + step]
        here = slice(i * step, (i + 1) * step)
        copies[i][0].wait()
        part = dot(x, wg[here, :], ((1,), (0,)))
        gate = part if gate is None else gate + part
        copies[i][1].wait()
        part = dot(x, wu[here, :], ((1,), (0,)))
        up = part if up is None else up + part
        copies[i][2].wait()
        part = dot(dy, wd[:, here], ((1,), (1,)))
        raw = part if raw is None else raw + part
    prob = own_ref[:, 2 * half :].astype(F32)[:, :1]
    sigma = jax.nn.sigmoid(gate)
    act = gate * sigma
    hidden = (act * up).astype(BF16).astype(F32)
    row_part = jnp.sum(hidden * raw, axis=1, keepdims=True)
    grad_h = prob * raw
    g_up = (grad_h * act).astype(BF16)
    g_gate = (grad_h * up * sigma * (1.0 + gate * (1.0 - sigma))).astype(BF16)
    ph_ref[...] = (prob * hidden).astype(BF16)
    gg_ref[...] = g_gate
    gu_ref[...] = g_up
    row_part = jnp.broadcast_to(row_part, (row_part.shape[0], LANES))
    mine_ref[:, half:] = row_part
    send_ref[:, half:] = row_part.astype(BF16)
    for i in list(range(parts, 2 * parts)) + list(range(parts)):
        here = slice(i * step, (i + 1) * step)
        part = dot(g_gate, wg[here, :], ((1,), (1,))) + dot(g_up, wu[here, :], ((1,), (1,)))
        at = i % parts * step
        if i < parts:
            mine_ref[:, at : at + step] = part
        else:
            send_ref[:, at : at + step] = part.astype(BF16)


def expert_rows(core, own, other, gate_w, up_w, down_w):
    rows = own.shape[0]
    width, hid = gate_w.shape
    half = width // 2
    step = half // 2
    shape = jax.ShapeDtypeStruct
    return pl.pallas_call(
        functools.partial(expert_kernel, step),
        out_shape=[
            shape((rows, half + LANES), F32),
            shape((rows, half + LANES), BF16),
            shape((rows, hid), BF16),
            shape((rows, hid), BF16),
            shape((rows, hid), BF16),
        ],
        in_specs=[SMEM, VMEM, VMEM, ANY, ANY, ANY],
        out_specs=[VMEM] * 5,
        scratch_shapes=[
            pltpu.VMEM((width, hid), BF16),
            pltpu.VMEM((width, hid), BF16),
            pltpu.VMEM((hid, width), BF16),
            pltpu.SemaphoreType.DMA((3, width // step)),
        ],
        compiler_params=params(36),
        cost_estimate=cost(10 * rows * width * hid, 6 * width * hid + 4 * rows * width),
    )(core, own, other, gate_w, up_w, down_w)


def gather_kernel(top, cap, n, codes_ref, block_ref, *refs):
    parts, out = refs[:n], refs[-1]
    half = out.shape[1] - LANES
    hit, _ = hits(top, cap, block_ref[...], codes_ref[:, :1])
    ones = [jnp.where(h, 1.0, 0.0) for h in hit]
    rows = jnp.concatenate([r[...] for r in parts], axis=0)
    sums = dot(sum(ones).astype(BF16), rows[:, :half], ((0,), (0,)))
    lane = lax.broadcasted_iota(jnp.int32, (out.shape[0], LANES), 1)
    dp = jnp.zeros((out.shape[0], LANES), F32)
    for k in range(top):
        dp = jnp.where(lane == k, dot(ones[k].astype(BF16), rows[:, half:], ((0,), (0,))), dp)
    if len(refs) > n + 1:
        sums = sums + refs[n][:, :half].astype(F32)
        dp = dp + refs[n][:, half:].astype(F32)
    out[:, :half] = sums.astype(BF16)
    out[:, half:] = dp.astype(BF16)


def gather_tokens(codes, block, parts, came, top, cap):
    tok, wide = block.shape
    wide_out = parts[0].shape[1]
    n = len(parts)
    extra = [] if came is None else [came]
    whole = lambda a: pl.BlockSpec(a.shape, lambda i: (0, 0))
    tail = pl.BlockSpec((tok, LANES), lambda i: (0, wide // LANES - 1))
    return pl.pallas_call(
        functools.partial(gather_kernel, top, cap, n),
        out_shape=jax.ShapeDtypeStruct((tok, wide_out), BF16),
        grid=(1,),
        in_specs=[whole(codes), tail] + [whole(a) for a in parts] + [whole(a) for a in extra],
        out_specs=pl.BlockSpec((tok, wide_out), lambda i: (0, 0)),
        compiler_params=params(24),
        cost_estimate=cost(2 * tok * codes.shape[0] * wide_out, 6 * tok * wide_out),
    )(codes, block, *parts, *extra)


def weights_kernel(n, core_ref, *refs):
    x_own, x_other, dy_own, dy_other, ph, gg, gu = (refs[i * n : (i + 1) * n] for i in range(7))
    d_gate, d_up, d_down, own_x, own_dy = refs[7 * n :]
    rows = x_own[0].shape[0]

    def put(xs, dys):
        for k in range(n):
            own_x[k * rows : (k + 1) * rows, :] = xs[k][...]
            own_dy[k * rows : (k + 1) * rows, :] = dys[k][...]

    @pl.when(pl.program_id(0) == 0)
    def _():
        put(x_own, dy_own)

    @pl.when(pl.program_id(0) == 1)
    def _():
        put(x_other, dy_other)

    stack = lambda a: jnp.concatenate([r[...] for r in a], axis=0)
    x = own_x[...]
    d_gate[...] = dot(x, stack(gg), ((0,), (0,))).astype(BF16)
    d_up[...] = dot(x, stack(gu), ((0,), (0,))).astype(BF16)
    d_down[...] = dot(stack(ph), own_dy[...], ((0,), (0,))).astype(BF16)


def weight_gradients(core, owns, others, ph, gg, gu):
    n = len(owns)
    rows, hid = ph[0].shape
    half = (owns[0].shape[1] - LANES) // 2
    step = half // 2
    parts = half // step
    width = 2 * half
    own = lambda first: pl.BlockSpec((rows, step), lambda h, i, c: (0, first * parts + jnp.where(h == 0, i, parts - 1)))
    other = lambda first: pl.BlockSpec((rows, step), lambda h, i, c: (0, first * parts + jnp.where(h == 0, 0, i)))
    fixed = pl.BlockSpec((rows, hid), lambda h, i, c: (0, 0))
    place = lambda h, i, c: jnp.where(h == 0, c[0], 1 - c[0]) * parts + i
    shape = jax.ShapeDtypeStruct
    return pl.pallas_call(
        functools.partial(weights_kernel, n),
        out_shape=[shape((width, hid), BF16), shape((width, hid), BF16), shape((hid, width), BF16)],
        grid_spec=pltpu.PrefetchScalarGridSpec(
            num_scalar_prefetch=1,
            grid=(2, parts),
            in_specs=[own(0)] * n + [other(0)] * n + [own(1)] * n + [other(1)] * n + [fixed] * (3 * n),
            out_specs=[
                pl.BlockSpec((step, hid), lambda h, i, c: (place(h, i, c), 0)),
                pl.BlockSpec((step, hid), lambda h, i, c: (place(h, i, c), 0)),
                pl.BlockSpec((hid, step), lambda h, i, c: (0, place(h, i, c))),
            ],
            scratch_shapes=[pltpu.VMEM((n * rows, step), BF16)] * 2,
        ),
        compiler_params=params(48),
        cost_estimate=cost(6 * n * rows * width * hid, 6 * width * hid + 4 * n * rows * width),
    )(core, *owns, *others, *owns, *others, *ph, *gg, *gu)


def on_device(tokens, grad_out, routes, probs, w_gate, w_up, w_down):
    experts = lax.axis_size("expert")
    tok, width = tokens.shape
    top = routes.shape[1]
    cap = 3 * tok * top // experts
    plane = experts // RINGS
    half = width // 2
    me = lax.axis_index("expert")
    core_id = lax.axis_index("tensor")
    core = core_id.astype(jnp.int32).reshape(1)
    z, p = me // plane, me % plane
    weights = (w_gate[0], w_up[0], w_down[0])

    ring = [(i, (i + plane) % experts) for i in range(experts)]
    peers = [[(i, i // plane * plane + ((i % plane) ^ j)) for i in range(experts)] for j in range(plane)]
    swap = [(0, 1), (1, 0)]

    row = jnp.arange(plane * cap, dtype=jnp.int32)
    codes = (z * plane + (p ^ (row // cap))) * cap + row % cap
    codes = jnp.broadcast_to(codes.astype(F32)[:, None], (plane * cap, LANES))
    meet = lax.optimization_barrier

    def hop(rows):
        return lax.ppermute(rows, "expert", ring)

    def turn(rows):
        return lax.ppermute(rows, "tensor", swap)

    def exchange(parts):
        return [parts[0]] + [lax.ppermute(parts[j], "expert", peers[j]) for j in range(1, plane)]

    def joined(parts):
        return jnp.concatenate(parts, axis=0)

    def work(own, other):
        mine, send, *kept = expert_rows(core, own, other, *weights)
        return mine, send, kept

    def summed(mine, came):
        total = (mine + came.astype(F32)).astype(BF16)
        return [total[j * cap : (j + 1) * cap] for j in range(plane)]

    def gather(block, parts, came=None):
        return gather_tokens(codes, block, parts, came, top, cap)

    h0 = make_block(core, tokens, grad_out, routes, probs, experts)

    h1 = hop(h0)
    g0 = exchange(choose(codes, h0, top, cap))
    h1, g0 = meet((h1, g0))

    h2 = hop(h1)
    own0 = joined(g0)
    other0, s1 = meet((turn(own0), choose(codes, h1, top, cap)))
    g1 = exchange(s1)
    mine0, send0, w0 = work(own0, other0)
    h2, g1, mine0, send0, w0 = meet((h2, g1, mine0, send0, w0))

    h3 = hop(h2)
    own1 = joined(g1)
    other1, came0, s2 = meet((turn(own1), turn(send0), choose(codes, h2, top, cap)))
    g2 = exchange(s2)
    c0 = summed(mine0, came0)
    mine1, send1, w1 = work(own1, other1)
    h3, g2, c0, mine1, send1, w1 = meet((h3, g2, c0, mine1, send1, w1))

    own2 = joined(g2)
    other2, came1, s3 = meet((turn(own2), turn(send1), choose(codes, h3, top, cap)))
    g3 = exchange(s3)
    b1 = exchange(summed(mine1, came1))
    mine2, send2, w2 = work(own2, other2)
    g3, b1, mine2, send2, w2 = meet((g3, b1, mine2, send2, w2))

    own3 = joined(g3)
    other3, came2, t1 = meet((turn(own3), turn(send2), gather(h1, b1)))
    r1 = hop(t1)
    b2 = exchange(summed(mine2, came2))
    mine3, send3, w3 = work(own3, other3)
    r1, b2, mine3, send3, w3, c0 = meet((r1, b2, mine3, send3, w3, c0))

    came3, t2 = meet((turn(send3), gather(h2, b2, r1)))
    r2 = hop(t2)
    b3 = exchange(summed(mine3, came3))
    b0 = exchange(c0)
    grads = weight_gradients(core, (own0, own1, own2, own3), (other0, other1, other2, other3), *zip(w0, w1, w2, w3))
    r2, b3, b0, grads = meet((r2, b3, b0, grads))

    r3 = hop(gather(h3, b3, r2))
    total = gather(h0, b0, r3)

    partner = turn(total)
    first = jnp.where(core_id == 0, total, partner)
    second = jnp.where(core_id == 0, partner, total)
    d_tokens = jnp.concatenate([first[:, :half], second[:, :half]], axis=1)
    d_probs = first[:, half : half + top]
    d_gate, d_up, d_down = (g[None] for g in grads)
    return (d_tokens, d_probs, d_gate, d_up, d_down)


def solution(mesh):
    rows = P("expert", None)
    columns = P("expert", None, "tensor")
    down = P("expert", "tensor", None)
    return jax.shard_map(
        on_device,
        mesh=mesh,
        in_specs=(rows, rows, rows, rows, columns, columns, down),
        out_specs=(rows, rows, columns, columns, down),
        check_vma=False,
    )
```

```python
import functools

import jax
import jax.numpy as jnp
from jax import lax
from jax.experimental import pallas as pl
from jax.experimental.pallas import tpu as pltpu
from jax.sharding import PartitionSpec as P

BF16 = jnp.bfloat16
F32 = jnp.float32
LANES = 128
RINGS = 4
VMEM = pl.BlockSpec(memory_space=pltpu.VMEM)
SMEM = pl.BlockSpec(memory_space=pltpu.SMEM)
ANY = pl.BlockSpec(memory_space=pl.ANY)


def dot(a, b, dims):
    return lax.dot_general(a, b, (dims, ((), ())), preferred_element_type=F32)


def params(mib):
    return pltpu.CompilerParams(vmem_limit_bytes=mib * 2**20)


def cost(flops, nbytes):
    return pl.CostEstimate(flops=flops, bytes_accessed=nbytes, transcendentals=0)


CLAIM = 4 * 10**10


def block_kernel(core_ref, tok_hbm, dy_hbm, routes_hbm, probs_hbm, out_ref, routes_ref, probs_ref, sems):
    top, tok = routes_ref.shape
    half = tok_hbm.shape[1] // 2
    mine = pl.ds(pl.multiple_of(core_ref[0] * half, LANES), half)
    copies = [
        pltpu.make_async_copy(routes_hbm, routes_ref, sems.at[2]),
        pltpu.make_async_copy(probs_hbm, probs_ref, sems.at[3]),
        pltpu.make_async_copy(tok_hbm.at[:, mine], out_ref.at[:, pl.ds(0, half)], sems.at[0]),
        pltpu.make_async_copy(dy_hbm.at[:, mine], out_ref.at[:, pl.ds(half, half)], sems.at[1]),
    ]
    for copy in copies:
        copy.start()
    copies[0].wait()
    copies[1].wait()
    expert = lax.broadcasted_iota(jnp.int32, (LANES, tok), 0)
    row = lax.broadcasted_iota(jnp.int32, (tok, tok), 0)
    col = lax.broadcasted_iota(jnp.int32, (tok, tok), 1)
    hot = [expert == routes_ref[k : k + 1, :] for k in range(top)]
    named = sum(jnp.where(h, 1.0, 0.0) for h in hot).astype(BF16)
    before = jnp.where(row < col, 1.0, 0.0).astype(BF16)
    counts = dot(named, before, ((1,), (0,)))
    field = lax.broadcasted_iota(jnp.int32, (tok, LANES), 0)
    aux = jnp.zeros((tok, LANES), F32)
    for k in range(top):
        slot = jnp.sum(jnp.where(hot[k], counts, 0.0), axis=0, keepdims=True)
        aux = jnp.where(field == k, routes_ref[k : k + 1, :].astype(F32), aux)
        aux = jnp.where(field == top + k, slot, aux)
        aux = jnp.where(field == 2 * top + k, probs_ref[k : k + 1, :].astype(F32), aux)
    out_ref[:, 2 * half :] = aux.astype(BF16)
    copies[2].wait()
    copies[3].wait()


def make_block(core, tokens, grad_out, routes, probs):
    tok, width = tokens.shape
    return pl.pallas_call(
        block_kernel,
        out_shape=jax.ShapeDtypeStruct((tok, width + LANES), BF16),
        in_specs=[SMEM, ANY, ANY, ANY, ANY],
        out_specs=VMEM,
        scratch_shapes=[
            pltpu.VMEM(routes.T.shape, routes.dtype),
            pltpu.VMEM(probs.T.shape, probs.dtype),
            pltpu.SemaphoreType.DMA((4,)),
        ],
        compiler_params=params(56),
        cost_estimate=cost(2 * tok * tok * LANES, 4 * tok * width),
    )(core, tokens, grad_out, routes.T, probs.T)


def hits(top, cap, aux, codes):
    aux = aux[...].astype(F32)
    return [codes == aux[k : k + 1] * cap + aux[top + k : top + k + 1] for k in range(top)], aux


def choose_kernel(top, cap, waits, codes_ref, block_ref, *refs):
    outs = refs[waits:]
    tok, wide = block_ref.shape
    body = wide - LANES
    hit, aux = hits(top, cap, block_ref[:, body:], codes_ref[...])
    both = sum(jnp.where(h, 1.0, 0.0) for h in hit).astype(BF16)
    rows = dot(both, block_ref[:, :body], ((1,), (0,))).astype(BF16)
    prob = sum(jnp.where(hit[k], aux[2 * top + k : 2 * top + k + 1], 0.0) for k in range(top))
    prob = jnp.broadcast_to(jnp.sum(prob, axis=1, keepdims=True), (rows.shape[0], LANES)).astype(BF16)
    for j, out in enumerate(outs):
        out[:, :body] = rows[j * cap : (j + 1) * cap]
        out[:, body:] = prob[j * cap : (j + 1) * cap]


def choose(codes, block, waits, top, cap):
    rows, wide = codes.shape[0], block.shape[1]
    return pl.pallas_call(
        functools.partial(choose_kernel, top, cap, len(waits)),
        out_shape=[jax.ShapeDtypeStruct((cap, wide), BF16)] * (rows // cap),
        in_specs=[VMEM, VMEM] + [ANY] * len(waits),
        out_specs=[VMEM] * (rows // cap),
        compiler_params=params(12),
        cost_estimate=cost(CLAIM, 2 * wide * (rows + block.shape[0])),
    )(codes, block, *waits)


def expert_kernel(core_ref, own_ref, other_ref, wg, wu, wd, mine_ref, send_ref, ph_ref, gg_ref, gu_ref):
    half = own_ref.shape[1] // 2 // LANES * LANES
    sides = [pl.ds(pl.multiple_of(c * half, LANES), half) for c in (core_ref[0], 1 - core_ref[0])]
    gate = up = raw = 0.0
    for ref, side in zip((own_ref, other_ref), sides):
        x, dy = ref[:, :half], ref[:, half : 2 * half]
        gate = gate + dot(x, wg[side, :], ((1,), (0,)))
        up = up + dot(x, wu[side, :], ((1,), (0,)))
        raw = raw + dot(dy, wd[:, side], ((1,), (1,)))
    prob = own_ref[:, 2 * half :].astype(F32)[:, :1]
    sigma = jax.nn.sigmoid(gate)
    act = gate * sigma
    hidden = (act * up).astype(BF16).astype(F32)
    row_part = jnp.sum(hidden * raw, axis=1, keepdims=True)
    grad_h = prob * raw
    g_up = (grad_h * act).astype(BF16)
    g_gate = (grad_h * up * sigma * (1.0 + gate * (1.0 - sigma))).astype(BF16)
    ph_ref[...] = (prob * hidden).astype(BF16)
    gg_ref[...] = g_gate
    gu_ref[...] = g_up
    row_part = jnp.broadcast_to(row_part, (row_part.shape[0], LANES))
    mine_ref[:, half:] = row_part.astype(BF16).astype(F32)
    send_ref[:, half:] = row_part.astype(BF16)
    for ref, side in zip((mine_ref, send_ref), sides):
        part = dot(g_gate, wg[side, :], ((1,), (1,))) + dot(g_up, wu[side, :], ((1,), (1,)))
        ref[:, :half] = part.astype(ref.dtype)


def expert_rows(core, own, other, gate_w, up_w, down_w):
    rows = own.shape[0]
    width, hid = gate_w.shape
    half = width // 2
    shape = jax.ShapeDtypeStruct
    return pl.pallas_call(
        expert_kernel,
        out_shape=[shape((rows, half + LANES), F32), shape((rows, half + LANES), BF16)] + [shape((rows, hid), BF16)] * 3,
        in_specs=[SMEM] + [VMEM] * 5,
        out_specs=[VMEM] * 5,
        compiler_params=params(16),
        cost_estimate=cost(10 * rows * width * hid, 4 * rows * width),
    )(core, own, other, gate_w, up_w, down_w)


def gather_kernel(top, cap, n, adds, codes_ref, block_ref, *refs):
    parts, out = refs[:n], refs[-1]
    half = out.shape[1] - LANES
    hit, _ = hits(top, cap, block_ref, codes_ref[...])
    rows = jnp.concatenate([r[...] for r in parts], axis=0)
    both = sum(jnp.where(h, 1.0, 0.0) for h in hit).astype(BF16)
    sums = dot(both, rows[:, :half], ((0,), (0,)))
    row_dp = rows[:, half:].astype(F32)
    field = lax.broadcasted_iota(jnp.int32, (out.shape[0], LANES), 0)
    dp = jnp.zeros((out.shape[0], LANES), F32)
    for k in range(top):
        dp = jnp.where(field == k, jnp.sum(jnp.where(hit[k], row_dp, 0.0), axis=0, keepdims=True), dp)
    if adds:
        sums = sums + refs[n][:, :half].astype(F32)
        dp = dp + refs[n][:, half:].astype(F32)
    out[:, :half] = sums.astype(BF16)
    out[:, half:] = dp.astype(BF16)


def gather_tokens(codes, block, parts, came, waits, top, cap):
    tok, wide = block.shape
    wide_out = parts[0].shape[1]
    n = len(parts)
    extra = [] if came is None else [came]
    waits = list(waits)
    whole = lambda a: pl.BlockSpec(a.shape, lambda i: (0, 0))
    tail = pl.BlockSpec((tok, LANES), lambda i: (0, wide // LANES - 1))
    return pl.pallas_call(
        functools.partial(gather_kernel, top, cap, n, came is not None),
        out_shape=jax.ShapeDtypeStruct((tok, wide_out), BF16),
        grid=(1,),
        in_specs=[whole(codes), tail] + [whole(a) for a in parts + extra] + [ANY] * len(waits),
        out_specs=pl.BlockSpec((tok, wide_out), lambda i: (0, 0)),
        compiler_params=params(12),
        cost_estimate=cost(CLAIM, 6 * tok * wide_out),
    )(codes, block, *parts, *extra, *waits)


def weights_kernel(n, many, by_row, core_ref, *refs):
    sources = refs[:n], refs[n : 2 * n]
    factors = refs[2 * n : 2 * n + many * n]
    outs, data, fixed = refs[-2 - many : -2], refs[-2], refs[-1]
    rows, hid = factors[0].shape
    h, i = pl.program_id(0), pl.program_id(1)

    @pl.when((h == 0) & (i == 0))
    def _():
        for f in range(many):
            for k in range(n):
                part = factors[f * n + k][...]
                if by_row:
                    fixed[k * rows : (k + 1) * rows, f * hid : (f + 1) * hid] = part
                else:
                    fixed[:, k * rows : (k + 1) * rows] = part.astype(F32).T.astype(BF16)

    for side, source in enumerate(sources):

        @pl.when(h == side)
        def _():
            for k in range(n):
                data[k * rows : (k + 1) * rows, :] = source[k][...]

    if by_row:
        out = dot(data[...], fixed[...], ((0,), (0,)))
        for f in range(many):
            outs[f][...] = out[:, f * hid : (f + 1) * hid].astype(BF16)
    else:
        outs[0][...] = dot(fixed[...], data[...], ((1,), (0,))).astype(BF16)


def weight_gradients(core, owns, others, factors, by_row):
    n = len(owns)
    many = len(factors)
    rows, hid = factors[0][0].shape
    half = (owns[0].shape[1] - LANES) // 2
    step = half // 2
    parts = half // step
    width = 2 * half
    first = 0 if by_row else parts
    own = pl.BlockSpec((rows, step), lambda h, i, c: (0, first + jnp.where(h == 0, i, parts - 1)))
    other = pl.BlockSpec((rows, step), lambda h, i, c: (0, first + jnp.where(h == 0, 0, i)))
    whole = pl.BlockSpec((rows, hid), lambda h, i, c: (0, 0))
    place = lambda h, i, c: jnp.where(h == 0, c[0], 1 - c[0]) * parts + i
    if by_row:
        out, spec = (width, hid), pl.BlockSpec((step, hid), lambda h, i, c: (place(h, i, c), 0))
    else:
        out, spec = (hid, width), pl.BlockSpec((hid, step), lambda h, i, c: (0, place(h, i, c)))
    return pl.pallas_call(
        functools.partial(weights_kernel, n, many, by_row),
        out_shape=[jax.ShapeDtypeStruct(out, BF16)] * many,
        grid_spec=pltpu.PrefetchScalarGridSpec(
            num_scalar_prefetch=1,
            grid=(2, parts),
            in_specs=[own] * n + [other] * n + [whole] * (n * many),
            out_specs=[spec] * many,
            scratch_shapes=[
                pltpu.VMEM((n * rows, step), BF16),
                pltpu.VMEM((n * rows, many * hid) if by_row else (hid, n * rows), BF16),
            ],
        ),
        compiler_params=params(40),
        cost_estimate=cost(2 * many * n * rows * width * hid, 2 * many * width * hid + 2 * n * rows * width),
    )(core, *owns, *others, *(a for f in factors for a in f))


def place_kernel(core_ref, own_ref, other_ref, out_hbm, sems):
    half = out_hbm.shape[1] // 2
    copies = []
    for i, (ref, c) in enumerate(((own_ref, core_ref[0]), (other_ref, 1 - core_ref[0]))):
        there = pl.ds(pl.multiple_of(c * half, LANES), half)
        copies.append(pltpu.make_async_copy(ref.at[:, pl.ds(0, half)], out_hbm.at[:, there], sems.at[i]))
    for copy in copies:
        copy.start()
    for copy in copies:
        copy.wait()


def place_halves(core, own, other, width):
    return pl.pallas_call(
        place_kernel,
        out_shape=jax.ShapeDtypeStruct((own.shape[0], width), BF16),
        in_specs=[SMEM, VMEM, VMEM],
        out_specs=ANY,
        scratch_shapes=[pltpu.SemaphoreType.DMA((2,))],
        compiler_params=params(8),
        cost_estimate=cost(1, 4 * own.shape[0] * width),
    )(core, own, other)


def on_device(tokens, grad_out, routes, probs, w_gate, w_up, w_down):
    experts = lax.axis_size("expert")
    tok, width = tokens.shape
    top = routes.shape[1]
    cap = 3 * tok * top // experts
    plane = experts // RINGS
    half = width // 2
    me = lax.axis_index("expert")
    core_id = lax.axis_index("tensor")
    core = core_id.astype(jnp.int32).reshape(1)
    z, p = me // plane, me % plane
    weights = (w_gate[0], w_up[0], w_down[0])

    after = {0: 1, 1: 3, 3: 2, 2: 0}
    ring = [(i, after[i // plane] * plane + i % plane) for i in range(experts)]
    peers = [[(i, i // plane * plane + ((i % plane) ^ j)) for i in range(experts)] for j in range(plane)]
    swap = [(0, 1), (1, 0)]

    row = jnp.arange(plane * cap, dtype=jnp.int32)
    codes = (z * plane + (p ^ (row // cap))) * cap + row % cap
    codes = jnp.broadcast_to(codes.astype(F32)[:, None], (plane * cap, LANES))
    meet = lax.optimization_barrier

    def hop(rows):
        return lax.ppermute(rows, "expert", ring)

    def turn(rows):
        return lax.ppermute(rows, "tensor", swap)

    def exchange(parts):
        return [parts[0]] + [lax.ppermute(parts[j], "expert", peers[j]) for j in range(1, plane)]

    def joined(parts):
        return jnp.concatenate(parts, axis=0)

    def work(own, other):
        mine, send, *kept = expert_rows(core, own, other, *weights)
        return mine, send, kept

    def summed(mine, came):
        total = (mine + came.astype(F32)).astype(BF16)
        return [total[j * cap : (j + 1) * cap] for j in range(plane)]

    def picked(block, *waits):
        return list(choose(codes, block, waits, top, cap))

    def gather(block, parts, came=None, waits=()):
        return gather_tokens(codes, block, parts, came, waits, top, cap)

    h0 = make_block(core, tokens, grad_out, routes, probs)

    h1 = hop(h0)
    g0 = exchange(picked(h0))
    s1 = picked(h1, *g0)
    h1, s1, g0 = meet((h1, s1, g0))

    h2 = hop(h1)
    g1 = exchange(s1)
    own0 = joined(g0)
    other0 = turn(own0)
    mine0, send0, w0 = work(own0, other0)
    came0 = turn(send0)
    s2 = picked(h2, *g1)
    h2, s2, g1, mine0, came0, w0 = meet((h2, s2, g1, mine0, came0, w0))

    h3 = hop(h2)
    g2 = exchange(s2)
    own1 = joined(g1)
    other1 = turn(own1)
    mine1, send1, w1 = work(own1, other1)
    came1 = turn(send1)
    s3 = picked(h3, *g2)
    h3, s3, g2, mine1, came1, w1 = meet((h3, s3, g2, mine1, came1, w1))

    g3 = exchange(s3)
    b1 = exchange(summed(mine1, came1))
    own2 = joined(g2)
    other2 = turn(own2)
    mine2, send2, w2 = work(own2, other2)
    came2 = turn(send2)
    t1 = gather(h1, b1, waits=g3)
    g3, t1, mine2, came2, w2, mine0 = meet((g3, t1, mine2, came2, w2, mine0))

    r1 = hop(t1)
    b2 = exchange(summed(mine2, came2))
    own3 = joined(g3)
    other3 = turn(own3)
    mine3, send3, w3 = work(own3, other3)
    came3 = turn(send3)
    t2 = gather(h2, b2, r1)
    t2, mine3, came3, w3, mine0 = meet((t2, mine3, came3, w3, mine0))

    owns, others = (own0, own1, own2, own3), (other0, other1, other2, other3)
    ph, gg, gu = zip(w0, w1, w2, w3)
    r2 = hop(t2)
    b3 = exchange(summed(mine3, came3))
    (d_down,) = weight_gradients(core, owns, others, (ph,), False)
    c0 = summed(mine0, came0)
    t3 = gather(h3, b3, r2)
    t3, d_down, gg, gu, c0 = meet((t3, d_down, gg, gu, c0))

    r3 = hop(t3)
    b0 = exchange(c0)
    d_gate, d_up = weight_gradients(core, owns, others, (gg, gu), True)
    r3, b0, d_gate, d_up = meet((r3, b0, d_gate, d_up))
    total = gather(h0, b0, r3)

    d_tokens = place_halves(core, total, turn(total[:, :half]), width)
    d_probs = total[:top, half:].T
    return (d_tokens, d_probs, d_gate[None], d_up[None], d_down[None])


def solution(mesh):
    rows = P("expert", None)
    columns = P("expert", None, "tensor")
    down = P("expert", "tensor", None)
    return jax.shard_map(
        on_device,
        mesh=mesh,
        in_specs=(rows, rows, rows, rows, columns, columns, down),
        out_specs=(rows, rows, columns, columns, down),
        check_vma=False,
    )
```

```python
import functools

import jax
import jax.numpy as jnp
from jax import lax
from jax.experimental import pallas as pl
from jax.experimental.pallas import tpu as pltpu
from jax.sharding import PartitionSpec as P

BF16 = jnp.bfloat16
F32 = jnp.float32
LANES = 128
FIELDS = 16
RINGS = 4
VMEM = pl.BlockSpec(memory_space=pltpu.VMEM)
SMEM = pl.BlockSpec(memory_space=pltpu.SMEM)
ANY = pl.BlockSpec(memory_space=pl.ANY)


def dot(a, b, dims):
    return lax.dot_general(a, b, (dims, ((), ())), preferred_element_type=F32)


def params(mib):
    return pltpu.CompilerParams(vmem_limit_bytes=mib * 2**20)


def cost(flops, nbytes):
    return pl.CostEstimate(flops=flops, bytes_accessed=nbytes, transcendentals=0)


CLAIM = 4 * 10**10


def tiles(ref, tok):
    return jnp.concatenate([ref[i * tok : (i + 1) * tok, :] for i in range(ref.shape[0] // tok)], axis=1)


def put_tiles(ref, value):
    tok = value.shape[0]
    for i in range(value.shape[1] // LANES):
        ref[i * tok : (i + 1) * tok, :] = value[:, i * LANES : (i + 1) * LANES]


def block_kernel(core_ref, tok_hbm, dy_hbm, routes_hbm, probs_hbm, out_ref, tok_ref, routes_ref, probs_ref, sems):
    top, tok = routes_ref.shape
    half = tok_hbm.shape[1] // 2
    mine = pl.ds(pl.multiple_of(core_ref[0] * half, LANES), half)
    copies = [
        pltpu.make_async_copy(routes_hbm, routes_ref, sems.at[0]),
        pltpu.make_async_copy(probs_hbm, probs_ref, sems.at[1]),
        pltpu.make_async_copy(tok_hbm.at[:, mine], tok_ref.at[0], sems.at[2]),
        pltpu.make_async_copy(dy_hbm.at[:, mine], tok_ref.at[1], sems.at[3]),
    ]
    for copy in copies:
        copy.start()
    copies[0].wait()
    copies[1].wait()
    expert = lax.broadcasted_iota(jnp.int32, (LANES, tok), 0)
    row = lax.broadcasted_iota(jnp.int32, (tok, tok), 0)
    col = lax.broadcasted_iota(jnp.int32, (tok, tok), 1)
    hot = [expert == routes_ref[k : k + 1, :] for k in range(top)]
    named = sum(jnp.where(h, 1.0, 0.0) for h in hot).astype(BF16)
    before = jnp.where(row < col, 1.0, 0.0).astype(BF16)
    counts = dot(named, before, ((1,), (0,)))
    field = lax.broadcasted_iota(jnp.int32, (FIELDS, LANES), 0)
    aux = jnp.zeros((FIELDS, LANES), F32)
    for k in range(top):
        slot = jnp.sum(jnp.where(hot[k], counts, 0.0), axis=0, keepdims=True)
        aux = jnp.where(field == k, routes_ref[k : k + 1, :].astype(F32), aux)
        aux = jnp.where(field == top + k, slot, aux)
        aux = jnp.where(field == 2 * top + k, probs_ref[k : k + 1, :].astype(F32), aux)
    out_ref[2 * half * tok // LANES :, :] = aux.astype(BF16)
    for i in range(2):
        copies[2 + i].wait()
        put_tiles(out_ref.at[pl.ds(i * half * tok // LANES, half * tok // LANES), :], tok_ref[i])


def make_block(core, tokens, grad_out, routes, probs):
    tok, width = tokens.shape
    return pl.pallas_call(
        block_kernel,
        out_shape=jax.ShapeDtypeStruct((tok * width // LANES + FIELDS, LANES), BF16),
        in_specs=[SMEM, ANY, ANY, ANY, ANY],
        out_specs=VMEM,
        scratch_shapes=[
            pltpu.VMEM((2, tok, width // 2), BF16),
            pltpu.VMEM(routes.T.shape, routes.dtype),
            pltpu.VMEM(probs.T.shape, probs.dtype),
            pltpu.SemaphoreType.DMA((4,)),
        ],
        compiler_params=params(56),
        cost_estimate=cost(2 * tok * tok * LANES, 4 * tok * width),
    )(core, tokens, grad_out, routes.T, probs.T)


def hits(top, cap, aux, codes):
    aux = aux.astype(F32)
    return [codes == aux[k : k + 1] * cap + aux[top + k : top + k + 1] for k in range(top)], aux


def choose_kernel(top, cap, waits, codes_ref, block_ref, *refs):
    outs = refs[waits:]
    tall = block_ref.shape[0] - FIELDS
    body = outs[0].shape[1] - LANES
    hit, aux = hits(top, cap, block_ref[tall:, :], codes_ref[...])
    both = sum(jnp.where(h, 1.0, 0.0) for h in hit).astype(BF16)
    rows = dot(both, tiles(block_ref.at[pl.ds(0, tall), :], tall * LANES // body), ((1,), (0,))).astype(BF16)
    prob = sum(jnp.where(hit[k], aux[2 * top + k : 2 * top + k + 1], 0.0) for k in range(top))
    prob = jnp.broadcast_to(jnp.sum(prob, axis=1, keepdims=True), (rows.shape[0], LANES)).astype(BF16)
    for j, out in enumerate(outs):
        out[:, :body] = rows[j * cap : (j + 1) * cap]
        out[:, body:] = prob[j * cap : (j + 1) * cap]


def choose(codes, block, waits, tok, top, cap):
    rows = codes.shape[0]
    wide = (block.shape[0] - FIELDS) * LANES // tok + LANES
    return pl.pallas_call(
        functools.partial(choose_kernel, top, cap, len(waits)),
        out_shape=[jax.ShapeDtypeStruct((cap, wide), BF16)] * (rows // cap),
        in_specs=[VMEM, VMEM] + [ANY] * len(waits),
        out_specs=[VMEM] * (rows // cap),
        compiler_params=params(12),
        cost_estimate=cost(CLAIM, 2 * wide * (rows + tok)),
    )(codes, block, *waits)


def expert_kernel(core_ref, own_ref, other_ref, wg, wu, wd, mine_ref, send_ref, ph_ref, gg_ref, gu_ref):
    half = own_ref.shape[1] // 2 // LANES * LANES
    sides = [pl.ds(pl.multiple_of(c * half, LANES), half) for c in (core_ref[0], 1 - core_ref[0])]
    gate = up = raw = 0.0
    for ref, side in zip((own_ref, other_ref), sides):
        x, dy = ref[:, :half], ref[:, half : 2 * half]
        gate = gate + dot(x, wg[side, :], ((1,), (0,)))
        up = up + dot(x, wu[side, :], ((1,), (0,)))
        raw = raw + dot(dy, wd[:, side], ((1,), (1,)))
    prob = own_ref[:, 2 * half :].astype(F32)[:, :1]
    sigma = jax.nn.sigmoid(gate)
    act = gate * sigma
    hidden = (act * up).astype(BF16).astype(F32)
    row_part = jnp.sum(hidden * raw, axis=1, keepdims=True)
    grad_h = prob * raw
    g_up = (grad_h * act).astype(BF16)
    g_gate = (grad_h * up * sigma * (1.0 + gate * (1.0 - sigma))).astype(BF16)
    ph_ref[...] = (prob * hidden).astype(BF16)
    gg_ref[...] = g_gate
    gu_ref[...] = g_up
    row_part = jnp.broadcast_to(row_part, (row_part.shape[0], LANES))
    mine_ref[:, half:] = row_part.astype(BF16).astype(F32)
    send_ref[:, half:] = row_part.astype(BF16)
    for ref, side in zip((mine_ref, send_ref), sides):
        part = dot(g_gate, wg[side, :], ((1,), (1,))) + dot(g_up, wu[side, :], ((1,), (1,)))
        ref[:, :half] = part.astype(ref.dtype)


def expert_rows(core, own, other, gate_w, up_w, down_w):
    rows = own.shape[0]
    width, hid = gate_w.shape
    half = width // 2
    shape = jax.ShapeDtypeStruct
    return pl.pallas_call(
        expert_kernel,
        out_shape=[shape((rows, half + LANES), F32), shape((rows, half + LANES), BF16)] + [shape((rows, hid), BF16)] * 3,
        in_specs=[SMEM] + [VMEM] * 5,
        out_specs=[VMEM] * 5,
        compiler_params=params(16),
        cost_estimate=cost(10 * rows * width * hid, 4 * rows * width),
    )(core, own, other, gate_w, up_w, down_w)


def gather_kernel(top, cap, n, adds, flat, codes_ref, aux_ref, *refs):
    parts, out = refs[:n], refs[-1]
    half = parts[0].shape[1] - LANES
    hit, _ = hits(top, cap, aux_ref[...], codes_ref[...])
    tok = codes_ref.shape[1]
    rows = jnp.concatenate([r[...] for r in parts], axis=0)
    both = sum(jnp.where(h, 1.0, 0.0) for h in hit).astype(BF16)
    sums = dot(both, rows[:, :half], ((0,), (0,)))
    row_dp = rows[:, half:].astype(F32)
    field = lax.broadcasted_iota(jnp.int32, (FIELDS, LANES), 0)
    dp = jnp.zeros((FIELDS, LANES), F32)
    for k in range(top):
        dp = jnp.where(field == k, jnp.sum(jnp.where(hit[k], row_dp, 0.0), axis=0, keepdims=True), dp)
    tall = tok * half // LANES
    if adds:
        sums = sums + tiles(refs[n].at[pl.ds(0, tall), :], tok).astype(F32)
        dp = dp + refs[n][tall:, :].astype(F32)
    if flat:
        put_tiles(out, sums.astype(BF16))
        out[tall:, :] = dp.astype(BF16)
    else:
        refs[-2][...] = sums.astype(BF16)
        out[...] = dp.astype(BF16)


def gather_tokens(codes, block, parts, came, waits, top, cap, flat):
    tok = codes.shape[1]
    half = parts[0].shape[1] - LANES
    n = len(parts)
    extra = [] if came is None else [came]
    waits = list(waits)
    whole = lambda a: pl.BlockSpec(a.shape, lambda i: (0, 0))
    tail = pl.BlockSpec((FIELDS, LANES), lambda i: (block.shape[0] // FIELDS - 1, 0))
    out = jax.ShapeDtypeStruct((tok * half // LANES + FIELDS, LANES), BF16)
    if not flat:
        out = [jax.ShapeDtypeStruct((tok, half), BF16), jax.ShapeDtypeStruct((FIELDS, LANES), BF16)]
    return pl.pallas_call(
        functools.partial(gather_kernel, top, cap, n, came is not None, flat),
        out_shape=out,
        grid=(1,),
        in_specs=[whole(codes), tail] + [whole(a) for a in parts + extra] + [ANY] * len(waits),
        out_specs=jax.tree.map(whole, out),
        compiler_params=params(12),
        cost_estimate=cost(CLAIM, 6 * tok * half),
    )(codes, block, *parts, *extra, *waits)


def weights_kernel(n, many, by_row, core_ref, *refs):
    sources = refs[:n], refs[n : 2 * n]
    factors = refs[2 * n : 2 * n + many * n]
    outs, data, fixed = refs[-2 - many : -2], refs[-2], refs[-1]
    rows, hid = factors[0].shape
    h, i = pl.program_id(0), pl.program_id(1)

    @pl.when((h == 0) & (i == 0))
    def _():
        for f in range(many):
            for k in range(n):
                part = factors[f * n + k][...]
                if by_row:
                    fixed[k * rows : (k + 1) * rows, f * hid : (f + 1) * hid] = part
                else:
                    fixed[:, k * rows : (k + 1) * rows] = part.astype(F32).T.astype(BF16)

    for side, source in enumerate(sources):

        @pl.when(h == side)
        def _():
            for k in range(n):
                data[k * rows : (k + 1) * rows, :] = source[k][...]

    if by_row:
        out = dot(data[...], fixed[...], ((0,), (0,)))
        for f in range(many):
            outs[f][...] = out[:, f * hid : (f + 1) * hid].astype(BF16)
    else:
        outs[0][...] = dot(fixed[...], data[...], ((1,), (0,))).astype(BF16)


def weight_gradients(core, owns, others, factors, by_row):
    n = len(owns)
    many = len(factors)
    rows, hid = factors[0][0].shape
    half = (owns[0].shape[1] - LANES) // 2
    step = half // 2
    parts = half // step
    width = 2 * half
    first = 0 if by_row else parts
    own = pl.BlockSpec((rows, step), lambda h, i, c: (0, first + jnp.where(h == 0, i, parts - 1)))
    other = pl.BlockSpec((rows, step), lambda h, i, c: (0, first + jnp.where(h == 0, 0, i)))
    whole = pl.BlockSpec((rows, hid), lambda h, i, c: (0, 0))
    place = lambda h, i, c: jnp.where(h == 0, c[0], 1 - c[0]) * parts + i
    if by_row:
        out, spec = (width, hid), pl.BlockSpec((step, hid), lambda h, i, c: (place(h, i, c), 0))
    else:
        out, spec = (hid, width), pl.BlockSpec((hid, step), lambda h, i, c: (0, place(h, i, c)))
    return pl.pallas_call(
        functools.partial(weights_kernel, n, many, by_row),
        out_shape=[jax.ShapeDtypeStruct(out, BF16)] * many,
        grid_spec=pltpu.PrefetchScalarGridSpec(
            num_scalar_prefetch=1,
            grid=(2, parts),
            in_specs=[own] * n + [other] * n + [whole] * (n * many),
            out_specs=[spec] * many,
            scratch_shapes=[
                pltpu.VMEM((n * rows, step), BF16),
                pltpu.VMEM((n * rows, many * hid) if by_row else (hid, n * rows), BF16),
            ],
        ),
        compiler_params=params(40),
        cost_estimate=cost(rows * width * hid, 2 * n * rows * width),
    )(core, *owns, *others, *(a for f in factors for a in f))


def place_kernel(core_ref, own_ref, other_ref, out_hbm, sems):
    half = out_hbm.shape[1] // 2
    copies = []
    for i, (ref, c) in enumerate(((own_ref, core_ref[0]), (other_ref, 1 - core_ref[0]))):
        there = pl.ds(pl.multiple_of(c * half, LANES), half)
        copies.append(pltpu.make_async_copy(ref.at[:, pl.ds(0, half)], out_hbm.at[:, there], sems.at[i]))
    for copy in copies:
        copy.start()
    for copy in copies:
        copy.wait()


def place_halves(core, own, other, width):
    return pl.pallas_call(
        place_kernel,
        out_shape=jax.ShapeDtypeStruct((own.shape[0], width), BF16),
        in_specs=[SMEM, VMEM, VMEM],
        out_specs=ANY,
        scratch_shapes=[pltpu.SemaphoreType.DMA((2,))],
        compiler_params=params(8),
        cost_estimate=cost(1, 4 * own.shape[0] * width),
    )(core, own, other)


def on_device(tokens, grad_out, routes, probs, w_gate, w_up, w_down):
    experts = lax.axis_size("expert")
    tok, width = tokens.shape
    top = routes.shape[1]
    cap = 3 * tok * top // experts
    plane = experts // RINGS
    half = width // 2
    me = lax.axis_index("expert")
    core_id = lax.axis_index("tensor")
    core = core_id.astype(jnp.int32).reshape(1)
    z, p = me // plane, me % plane
    weights = (w_gate[0], w_up[0], w_down[0])

    after = {0: 1, 1: 3, 3: 2, 2: 0}
    ring = [(i, after[i // plane] * plane + i % plane) for i in range(experts)]
    peers = [[(i, i // plane * plane + ((i % plane) ^ j)) for i in range(experts)] for j in range(plane)]
    swap = [(0, 1), (1, 0)]

    row = jnp.arange(plane * cap, dtype=jnp.int32)
    codes = (z * plane + (p ^ (row // cap))) * cap + row % cap
    codes = jnp.broadcast_to(codes.astype(F32)[:, None], (plane * cap, LANES))
    meet = lax.optimization_barrier

    def hop(rows):
        return lax.ppermute(rows, "expert", ring)

    def turn(rows):
        return lax.ppermute(rows, "tensor", swap)

    def exchange(parts):
        return [parts[0]] + [lax.ppermute(parts[j], "expert", peers[j]) for j in range(1, plane)]

    def joined(parts):
        return jnp.concatenate(parts, axis=0)

    def work(own, other):
        mine, send, *kept = expert_rows(core, own, other, *weights)
        return mine, send, kept

    def summed(mine, came):
        total = (mine + came.astype(F32)).astype(BF16)
        return [total[j * cap : (j + 1) * cap] for j in range(plane)]

    def picked(block, *waits):
        return list(choose(codes, block, waits, tok, top, cap))

    def gather(block, parts, came=None, waits=(), flat=True):
        return gather_tokens(codes, block, parts, came, waits, top, cap, flat)

    h0 = make_block(core, tokens, grad_out, routes, probs)

    h1 = hop(h0)
    g0 = exchange(picked(h0))
    s1 = picked(h1, *g0)
    h1, s1, g0 = meet((h1, s1, g0))

    h2 = hop(h1)
    g1 = exchange(s1)
    own0 = joined(g0)
    other0 = turn(own0)
    mine0, send0, w0 = work(own0, other0)
    came0 = turn(send0)
    s2 = picked(h2, *g1)
    h2, s2, g1, mine0, came0, w0 = meet((h2, s2, g1, mine0, came0, w0))

    h3 = hop(h2)
    g2 = exchange(s2)
    own1 = joined(g1)
    other1 = turn(own1)
    mine1, send1, w1 = work(own1, other1)
    came1 = turn(send1)
    s3 = picked(h3, *g2)
    h3, s3, g2, mine1, came1, w1 = meet((h3, s3, g2, mine1, came1, w1))

    g3 = exchange(s3)
    b1 = exchange(summed(mine1, came1))
    own2 = joined(g2)
    other2 = turn(own2)
    mine2, send2, w2 = work(own2, other2)
    c2 = summed(mine2, turn(send2))
    t1 = gather(h1, b1, waits=g3)
    g3, t1, c2, w2, mine0 = meet((g3, t1, c2, w2, mine0))

    r1 = hop(t1)
    b2 = exchange(c2)
    own3 = joined(g3)
    other3 = turn(own3)
    mine3, send3, w3 = work(own3, other3)
    came3 = turn(send3)
    t2 = gather(h2, b2, r1)
    t2, mine3, came3, w3, mine0 = meet((t2, mine3, came3, w3, mine0))

    owns, others = (own0, own1, own2, own3), (other0, other1, other2, other3)
    ph, gg, gu = zip(w0, w1, w2, w3)
    r2 = hop(t2)
    b3 = exchange(summed(mine3, came3))
    (d_down,) = weight_gradients(core, owns, others, (ph,), False)
    c0 = summed(mine0, came0)
    t3 = gather(h3, b3, r2)
    t3, d_down, gg, gu, c0 = meet((t3, d_down, gg, gu, c0))

    r3 = hop(t3)
    b0 = exchange(c0)
    d_gate, d_up = weight_gradients(core, owns, others, (gg, gu), True)
    r3, b0, d_gate, d_up = meet((r3, b0, d_gate, d_up))
    total, dp = gather(h0, b0, r3, flat=False)

    d_tokens = place_halves(core, total, turn(total), width)
    d_probs = dp[:top, :].T
    return (d_tokens, d_probs, d_gate[None], d_up[None], d_down[None])


def solution(mesh):
    rows = P("expert", None)
    columns = P("expert", None, "tensor")
    down = P("expert", "tensor", None)
    return jax.shard_map(
        on_device,
        mesh=mesh,
        in_specs=(rows, rows, rows, rows, columns, columns, down),
        out_specs=(rows, rows, columns, columns, down),
        check_vma=False,
    )
```

```python
import functools

import jax
import jax.numpy as jnp
from jax import lax
from jax.experimental import pallas as pl
from jax.experimental.pallas import tpu as pltpu
from jax.sharding import PartitionSpec as P

BF16 = jnp.bfloat16
F32 = jnp.float32
LANES = 128
FIELDS = 16
RINGS = 4
VMEM = pl.BlockSpec(memory_space=pltpu.VMEM)
SMEM = pl.BlockSpec(memory_space=pltpu.SMEM)
ANY = pl.BlockSpec(memory_space=pl.ANY)


def dot(a, b, dims):
    return lax.dot_general(a, b, (dims, ((), ())), preferred_element_type=F32)


def params(mib):
    return pltpu.CompilerParams(vmem_limit_bytes=mib * 2**20)


def cost(flops, nbytes):
    return pl.CostEstimate(flops=flops, bytes_accessed=nbytes, transcendentals=0)


CLAIM = 4 * 10**10


def tiles(ref, tok):
    return jnp.concatenate([ref[i * tok : (i + 1) * tok, :] for i in range(ref.shape[0] // tok)], axis=1)


def put_tiles(ref, value):
    tok = value.shape[0]
    for i in range(value.shape[1] // LANES):
        ref[i * tok : (i + 1) * tok, :] = value[:, i * LANES : (i + 1) * LANES]


def block_kernel(core_ref, tok_hbm, dy_hbm, routes_hbm, probs_hbm, out_ref, tok_ref, routes_ref, probs_ref, sems):
    top, tok = routes_ref.shape
    half = tok_hbm.shape[1] // 2
    mine = pl.ds(pl.multiple_of(core_ref[0] * half, LANES), half)
    copies = [
        pltpu.make_async_copy(routes_hbm, routes_ref, sems.at[0]),
        pltpu.make_async_copy(probs_hbm, probs_ref, sems.at[1]),
        pltpu.make_async_copy(tok_hbm.at[:, mine], tok_ref.at[0], sems.at[2]),
        pltpu.make_async_copy(dy_hbm.at[:, mine], tok_ref.at[1], sems.at[3]),
    ]
    for copy in copies:
        copy.start()
    copies[0].wait()
    copies[1].wait()
    expert = lax.broadcasted_iota(jnp.int32, (LANES, tok), 0)
    row = lax.broadcasted_iota(jnp.int32, (tok, tok), 0)
    col = lax.broadcasted_iota(jnp.int32, (tok, tok), 1)
    hot = [expert == routes_ref[k : k + 1, :] for k in range(top)]
    named = sum(jnp.where(h, 1.0, 0.0) for h in hot).astype(BF16)
    before = jnp.where(row < col, 1.0, 0.0).astype(BF16)
    counts = dot(named, before, ((1,), (0,)))
    field = lax.broadcasted_iota(jnp.int32, (FIELDS, LANES), 0)
    aux = jnp.zeros((FIELDS, LANES), F32)
    for k in range(top):
        slot = jnp.sum(jnp.where(hot[k], counts, 0.0), axis=0, keepdims=True)
        aux = jnp.where(field == k, routes_ref[k : k + 1, :].astype(F32), aux)
        aux = jnp.where(field == top + k, slot, aux)
        aux = jnp.where(field == 2 * top + k, probs_ref[k : k + 1, :].astype(F32), aux)
    out_ref[2 * half * tok // LANES :, :] = aux.astype(BF16)
    for i in range(2):
        copies[2 + i].wait()
        put_tiles(out_ref.at[pl.ds(i * half * tok // LANES, half * tok // LANES), :], tok_ref[i])


def make_block(core, tokens, grad_out, routes, probs):
    tok, width = tokens.shape
    return pl.pallas_call(
        block_kernel,
        out_shape=jax.ShapeDtypeStruct((tok * width // LANES + FIELDS, LANES), BF16),
        in_specs=[SMEM, ANY, ANY, ANY, ANY],
        out_specs=VMEM,
        scratch_shapes=[
            pltpu.VMEM((2, tok, width // 2), BF16),
            pltpu.VMEM(routes.T.shape, routes.dtype),
            pltpu.VMEM(probs.T.shape, probs.dtype),
            pltpu.SemaphoreType.DMA((4,)),
        ],
        compiler_params=params(56),
        cost_estimate=cost(2 * tok * tok * LANES, 4 * tok * width),
    )(core, tokens, grad_out, routes.T, probs.T)


def hits(top, cap, aux, codes):
    aux = aux.astype(F32)
    return [codes == aux[k : k + 1] * cap + aux[top + k : top + k + 1] for k in range(top)], aux


def choose_kernel(top, cap, waits, codes_ref, block_ref, *refs):
    outs = refs[waits:]
    tall = block_ref.shape[0] - FIELDS
    body = outs[0].shape[1] - LANES
    hit, aux = hits(top, cap, block_ref[tall:, :], codes_ref[...])
    both = sum(jnp.where(h, 1.0, 0.0) for h in hit).astype(BF16)
    rows = dot(both, tiles(block_ref.at[pl.ds(0, tall), :], tall * LANES // body), ((1,), (0,))).astype(BF16)
    prob = sum(jnp.where(hit[k], aux[2 * top + k : 2 * top + k + 1], 0.0) for k in range(top))
    prob = jnp.broadcast_to(jnp.sum(prob, axis=1, keepdims=True), (rows.shape[0], LANES)).astype(BF16)
    for j, out in enumerate(outs):
        out[:, :body] = rows[j * cap : (j + 1) * cap]
        out[:, body:] = prob[j * cap : (j + 1) * cap]


def choose(codes, block, waits, tok, top, cap):
    rows = codes.shape[0]
    wide = (block.shape[0] - FIELDS) * LANES // tok + LANES
    return pl.pallas_call(
        functools.partial(choose_kernel, top, cap, len(waits)),
        out_shape=[jax.ShapeDtypeStruct((cap, wide), BF16)] * (rows // cap),
        in_specs=[VMEM, VMEM] + [ANY] * len(waits),
        out_specs=[VMEM] * (rows // cap),
        compiler_params=params(12),
        cost_estimate=cost(CLAIM, 2 * wide * (rows + tok)),
    )(codes, block, *waits)


def expert_kernel(core_ref, own_ref, other_ref, wg, wu, wd, mine_ref, send_ref, ph_ref, gg_ref, gu_ref):
    half = own_ref.shape[1] // 2 // LANES * LANES
    sides = [pl.ds(pl.multiple_of(c * half, LANES), half) for c in (core_ref[0], 1 - core_ref[0])]
    gate = up = raw = 0.0
    for ref, side in zip((own_ref, other_ref), sides):
        x, dy = ref[:, :half], ref[:, half : 2 * half]
        gate = gate + dot(x, wg[side, :], ((1,), (0,)))
        up = up + dot(x, wu[side, :], ((1,), (0,)))
        raw = raw + dot(dy, wd[:, side], ((1,), (1,)))
    prob = own_ref[:, 2 * half :].astype(F32)[:, :1]
    sigma = jax.nn.sigmoid(gate)
    act = gate * sigma
    hidden = (act * up).astype(BF16).astype(F32)
    row_part = jnp.sum(hidden * raw, axis=1, keepdims=True)
    grad_h = prob * raw
    g_up = (grad_h * act).astype(BF16)
    g_gate = (grad_h * up * sigma * (1.0 + gate * (1.0 - sigma))).astype(BF16)
    ph_ref[...] = (prob * hidden).astype(BF16)
    gg_ref[...] = g_gate
    gu_ref[...] = g_up
    row_part = jnp.broadcast_to(row_part, (row_part.shape[0], LANES))
    mine_ref[:, half:] = row_part.astype(BF16).astype(F32)
    send_ref[:, half:] = row_part.astype(BF16)
    for ref, side in zip((mine_ref, send_ref), sides):
        part = dot(g_gate, wg[side, :], ((1,), (1,))) + dot(g_up, wu[side, :], ((1,), (1,)))
        ref[:, :half] = part.astype(ref.dtype)


def expert_rows(core, own, other, gate_w, up_w, down_w):
    rows = own.shape[0]
    width, hid = gate_w.shape
    half = width // 2
    shape = jax.ShapeDtypeStruct
    return pl.pallas_call(
        expert_kernel,
        out_shape=[shape((rows, half + LANES), F32), shape((rows, half + LANES), BF16)] + [shape((rows, hid), BF16)] * 3,
        in_specs=[SMEM] + [VMEM] * 5,
        out_specs=[VMEM] * 5,
        compiler_params=params(16),
        cost_estimate=cost(10 * rows * width * hid, 4 * rows * width),
    )(core, own, other, gate_w, up_w, down_w)


def gather_kernel(top, cap, n, adds, flat, codes_ref, aux_ref, *refs):
    parts, out = refs[:n], refs[-1]
    half = parts[0].shape[1] - LANES
    hit, _ = hits(top, cap, aux_ref[...], codes_ref[...])
    tok = codes_ref.shape[1]
    rows = jnp.concatenate([r[...] for r in parts], axis=0)
    both = sum(jnp.where(h, 1.0, 0.0) for h in hit).astype(BF16)
    sums = dot(both, rows[:, :half], ((0,), (0,)))
    row_dp = rows[:, half:].astype(F32)
    field = lax.broadcasted_iota(jnp.int32, (FIELDS, LANES), 0)
    dp = jnp.zeros((FIELDS, LANES), F32)
    for k in range(top):
        dp = jnp.where(field == k, jnp.sum(jnp.where(hit[k], row_dp, 0.0), axis=0, keepdims=True), dp)
    tall = tok * half // LANES
    if adds:
        sums = sums + tiles(refs[n].at[pl.ds(0, tall), :], tok).astype(F32)
        dp = dp + refs[n][tall:, :].astype(F32)
    if flat:
        put_tiles(out, sums.astype(BF16))
        out[tall:, :] = dp.astype(BF16)
    else:
        refs[-2][...] = sums.astype(BF16)
        out[...] = dp.astype(BF16)


def gather_tokens(codes, block, parts, came, waits, top, cap, flat):
    tok = codes.shape[1]
    half = parts[0].shape[1] - LANES
    n = len(parts)
    extra = [] if came is None else [came]
    waits = list(waits)
    whole = lambda a: pl.BlockSpec(a.shape, lambda i: (0, 0))
    tail = pl.BlockSpec((FIELDS, LANES), lambda i: (block.shape[0] // FIELDS - 1, 0))
    out = jax.ShapeDtypeStruct((tok * half // LANES + FIELDS, LANES), BF16)
    if not flat:
        out = [jax.ShapeDtypeStruct((tok, half), BF16), jax.ShapeDtypeStruct((FIELDS, LANES), BF16)]
    return pl.pallas_call(
        functools.partial(gather_kernel, top, cap, n, came is not None, flat),
        out_shape=out,
        grid=(1,),
        in_specs=[whole(codes), tail] + [whole(a) for a in parts + extra] + [ANY] * len(waits),
        out_specs=jax.tree.map(whole, out),
        compiler_params=params(12),
        cost_estimate=cost(CLAIM, 6 * tok * half),
    )(codes, block, *parts, *extra, *waits)


def weights_kernel(n, many, by_row, step, core_ref, *refs):
    sides = refs[:n], refs[n : 2 * n]
    factors = refs[2 * n : 2 * n + many * n]
    outs, (fixed, held, sems) = refs[2 * n + many * n : -3], refs[-3:]
    rows, hid = factors[0].shape
    half = sides[0][0].shape[1] // 2 // LANES * LANES
    parts = half // step
    first = 0 if by_row else half
    for f in range(many):
        for k in range(n):
            part = factors[f * n + k][...]
            if by_row:
                fixed[k * rows : (k + 1) * rows, f * hid : (f + 1) * hid] = part
            else:
                fixed[:, k * rows : (k + 1) * rows] = part.astype(F32).T.astype(BF16)
    copies = []
    for i in range(2 * parts):
        side, at = i // parts, first + i % parts * step
        data = jnp.concatenate([r[:, at : at + step] for r in sides[side]], axis=0)
        out = dot(data, fixed[...], ((0,), (0,))) if by_row else dot(fixed[...], data, ((1,), (0,)))
        c = core_ref[0] if side == 0 else 1 - core_ref[0]
        there = pl.ds(pl.multiple_of(c * half + i % parts * step, LANES), step)
        if i >= 2:
            for copy in copies[i - 2]:
                copy.wait()
        copies.append([])
        for f in range(many):
            if by_row:
                held[i % 2, f] = out[:, f * hid : (f + 1) * hid].astype(BF16)
                target = outs[f].at[there, :]
            else:
                held[i % 2, f] = out.astype(BF16)
                target = outs[f].at[:, there]
            copies[i].append(pltpu.make_async_copy(held.at[i % 2, f], target, sems.at[i % 2, f]))
            copies[i][f].start()
    for group in copies[-2:]:
        for copy in group:
            copy.wait()


def weight_gradients(core, owns, others, factors, by_row):
    n = len(owns)
    many = len(factors)
    rows, hid = factors[0][0].shape
    half = (owns[0].shape[1] - LANES) // 2
    step = half // 2
    width = 2 * half
    tile = (step, hid) if by_row else (hid, step)
    return pl.pallas_call(
        functools.partial(weights_kernel, n, many, by_row, step),
        out_shape=[jax.ShapeDtypeStruct((width, hid) if by_row else (hid, width), BF16)] * many,
        in_specs=[SMEM] + [VMEM] * (2 * n + many * n),
        out_specs=[ANY] * many,
        scratch_shapes=[
            pltpu.VMEM((n * rows, many * hid) if by_row else (hid, n * rows), BF16),
            pltpu.VMEM((2, many) + tile, BF16),
            pltpu.SemaphoreType.DMA((2, many)),
        ],
        compiler_params=params(24),
        cost_estimate=cost(rows * width * hid, 2 * n * rows * width),
    )(core, *owns, *others, *(a for f in factors for a in f))


def place_kernel(core_ref, own_ref, other_ref, out_hbm, sems):
    half = out_hbm.shape[1] // 2
    copies = []
    for i, (ref, c) in enumerate(((own_ref, core_ref[0]), (other_ref, 1 - core_ref[0]))):
        there = pl.ds(pl.multiple_of(c * half, LANES), half)
        copies.append(pltpu.make_async_copy(ref.at[:, pl.ds(0, half)], out_hbm.at[:, there], sems.at[i]))
    for copy in copies:
        copy.start()
    for copy in copies:
        copy.wait()


def place_halves(core, own, other, width):
    return pl.pallas_call(
        place_kernel,
        out_shape=jax.ShapeDtypeStruct((own.shape[0], width), BF16),
        in_specs=[SMEM, VMEM, VMEM],
        out_specs=ANY,
        scratch_shapes=[pltpu.SemaphoreType.DMA((2,))],
        compiler_params=params(8),
        cost_estimate=cost(1, 4 * own.shape[0] * width),
    )(core, own, other)


def on_device(tokens, grad_out, routes, probs, w_gate, w_up, w_down):
    experts = lax.axis_size("expert")
    tok, width = tokens.shape
    top = routes.shape[1]
    cap = 3 * tok * top // experts
    plane = experts // RINGS
    half = width // 2
    me = lax.axis_index("expert")
    core_id = lax.axis_index("tensor")
    core = core_id.astype(jnp.int32).reshape(1)
    z, p = me // plane, me % plane
    weights = (w_gate[0], w_up[0], w_down[0])

    after = {0: 1, 1: 3, 3: 2, 2: 0}
    ring = [(i, after[i // plane] * plane + i % plane) for i in range(experts)]
    peers = [[(i, i // plane * plane + ((i % plane) ^ j)) for i in range(experts)] for j in range(plane)]
    swap = [(0, 1), (1, 0)]

    row = jnp.arange(plane * cap, dtype=jnp.int32)
    codes = (z * plane + (p ^ (row // cap))) * cap + row % cap
    codes = jnp.broadcast_to(codes.astype(F32)[:, None], (plane * cap, LANES))
    meet = lax.optimization_barrier

    def hop(rows):
        return lax.ppermute(rows, "expert", ring)

    def turn(rows):
        return lax.ppermute(rows, "tensor", swap)

    def exchange(parts):
        return [parts[0]] + [lax.ppermute(parts[j], "expert", peers[j]) for j in range(1, plane)]

    def joined(parts):
        return jnp.concatenate(parts, axis=0)

    def work(own, other):
        mine, send, *kept = expert_rows(core, own, other, *weights)
        return mine, send, kept

    def summed(mine, came):
        total = (mine + came.astype(F32)).astype(BF16)
        return [total[j * cap : (j + 1) * cap] for j in range(plane)]

    def picked(block, *waits):
        return list(choose(codes, block, waits, tok, top, cap))

    def gather(block, parts, came=None, waits=(), flat=True):
        return gather_tokens(codes, block, parts, came, waits, top, cap, flat)

    h0 = make_block(core, tokens, grad_out, routes, probs)

    h1 = hop(h0)
    g0 = exchange(picked(h0))
    s1 = picked(h1, *g0)
    h1, s1, g0 = meet((h1, s1, g0))

    h2 = hop(h1)
    g1 = exchange(s1)
    own0 = joined(g0)
    other0 = turn(own0)
    mine0, send0, w0 = work(own0, other0)
    came0 = turn(send0)
    s2 = picked(h2, *g1)
    h2, s2, g1, mine0, came0, w0 = meet((h2, s2, g1, mine0, came0, w0))

    h3 = hop(h2)
    g2 = exchange(s2)
    own1 = joined(g1)
    other1 = turn(own1)
    mine1, send1, w1 = work(own1, other1)
    came1 = turn(send1)
    s3 = picked(h3, *g2)
    h3, s3, g2, mine1, came1, w1 = meet((h3, s3, g2, mine1, came1, w1))

    g3 = exchange(s3)
    b1 = exchange(summed(mine1, came1))
    own2 = joined(g2)
    other2 = turn(own2)
    mine2, send2, w2 = work(own2, other2)
    t1 = gather(h1, b1, waits=(*g3, send2))
    g3, t1, mine2, send2, w2, mine0 = meet((g3, t1, mine2, send2, w2, mine0))

    r1 = hop(t1)
    b2 = exchange(summed(mine2, turn(send2)))
    own3 = joined(g3)
    other3 = turn(own3)
    mine3, send3, w3 = work(own3, other3)
    came3 = turn(send3)
    t2 = gather(h2, b2, r1)
    t2, mine3, came3, w3, mine0 = meet((t2, mine3, came3, w3, mine0))

    owns, others = (own0, own1, own2, own3), (other0, other1, other2, other3)
    ph, gg, gu = zip(w0, w1, w2, w3)
    r2 = hop(t2)
    b3 = exchange(summed(mine3, came3))
    (d_down,) = weight_gradients(core, owns, others, (ph,), False)
    c0 = summed(mine0, came0)
    t3 = gather(h3, b3, r2)
    t3, d_down, gg, gu, c0 = meet((t3, d_down, gg, gu, c0))

    r3 = hop(t3)
    b0 = exchange(c0)
    d_gate, d_up = weight_gradients(core, owns, others, (gg, gu), True)
    r3, b0, d_gate, d_up = meet((r3, b0, d_gate, d_up))
    total, dp = gather(h0, b0, r3, flat=False)

    d_tokens = place_halves(core, total, turn(total), width)
    d_probs = dp[:top, :].T
    return (d_tokens, d_probs, d_gate[None], d_up[None], d_down[None])


def solution(mesh):
    rows = P("expert", None)
    columns = P("expert", None, "tensor")
    down = P("expert", "tensor", None)
    return jax.shard_map(
        on_device,
        mesh=mesh,
        in_specs=(rows, rows, rows, rows, columns, columns, down),
        out_specs=(rows, rows, columns, columns, down),
        check_vma=False,
    )
```

```python
import functools

import jax
import jax.numpy as jnp
from jax import lax
from jax.experimental import pallas as pl
from jax.experimental.pallas import tpu as pltpu
from jax.sharding import PartitionSpec as P

BF16 = jnp.bfloat16
F32 = jnp.float32
LANES = 128
FIELDS = 16
RINGS = 4
VMEM = pl.BlockSpec(memory_space=pltpu.VMEM)
SMEM = pl.BlockSpec(memory_space=pltpu.SMEM)
ANY = pl.BlockSpec(memory_space=pl.ANY)


def dot(a, b, dims):
    return lax.dot_general(a, b, (dims, ((), ())), preferred_element_type=F32)


def params(mib):
    return pltpu.CompilerParams(vmem_limit_bytes=mib * 2**20)


def cost(flops, nbytes):
    return pl.CostEstimate(flops=flops, bytes_accessed=nbytes, transcendentals=0)


CLAIM = 4 * 10**10


def tiles(ref, tok):
    return jnp.concatenate([ref[i * tok : (i + 1) * tok, :] for i in range(ref.shape[0] // tok)], axis=1)


def put_tiles(ref, value):
    tok = value.shape[0]
    for i in range(value.shape[1] // LANES):
        ref[i * tok : (i + 1) * tok, :] = value[:, i * LANES : (i + 1) * LANES]


def block_kernel(tok_ref, dy_ref, routes_ref, probs_ref, out_ref):
    top, tok = routes_ref.shape
    tall = tok_ref.shape[1] * tok // LANES
    expert = lax.broadcasted_iota(jnp.int32, (LANES, tok), 0)
    row = lax.broadcasted_iota(jnp.int32, (tok, tok), 0)
    col = lax.broadcasted_iota(jnp.int32, (tok, tok), 1)
    hot = [expert == routes_ref[k : k + 1, :] for k in range(top)]
    named = sum(jnp.where(h, 1.0, 0.0) for h in hot).astype(BF16)
    before = jnp.where(row < col, 1.0, 0.0).astype(BF16)
    counts = dot(named, before, ((1,), (0,)))
    field = lax.broadcasted_iota(jnp.int32, (FIELDS, LANES), 0)
    aux = jnp.zeros((FIELDS, LANES), F32)
    for k in range(top):
        slot = jnp.sum(jnp.where(hot[k], counts, 0.0), axis=0, keepdims=True)
        aux = jnp.where(field == k, routes_ref[k : k + 1, :].astype(F32), aux)
        aux = jnp.where(field == top + k, slot, aux)
        aux = jnp.where(field == 2 * top + k, probs_ref[k : k + 1, :].astype(F32), aux)
    for i, ref in enumerate((tok_ref, dy_ref)):
        put_tiles(out_ref.at[pl.ds(i * tall, tall), :], ref[...])
    out_ref[2 * tall :, :] = aux.astype(BF16)


def make_block(core, tokens, grad_out, routes, probs):
    tok, width = tokens.shape
    half = width // 2
    mine = [lax.dynamic_slice_in_dim(a, core[0] * half, half, axis=1) for a in (tokens, grad_out)]
    return pl.pallas_call(
        block_kernel,
        out_shape=jax.ShapeDtypeStruct((tok * width // LANES + FIELDS, LANES), BF16),
        in_specs=[VMEM] * 4,
        out_specs=VMEM,
        compiler_params=params(8),
        cost_estimate=cost(2 * tok * tok * LANES, 4 * tok * width),
    )(*mine, routes.T, probs.T)


def hits(top, cap, aux, codes):
    aux = aux.astype(F32)
    return [codes == aux[k : k + 1] * cap + aux[top + k : top + k + 1] for k in range(top)], aux


def choose_kernel(top, cap, waits, codes_ref, block_ref, *refs):
    outs = refs[waits:]
    tall = block_ref.shape[0] - FIELDS
    body = outs[0].shape[1] - LANES
    hit, aux = hits(top, cap, block_ref[tall:, :], codes_ref[...])
    both = sum(jnp.where(h, 1.0, 0.0) for h in hit).astype(BF16)
    rows = dot(both, tiles(block_ref.at[pl.ds(0, tall), :], tall * LANES // body), ((1,), (0,))).astype(BF16)
    prob = sum(jnp.where(hit[k], aux[2 * top + k : 2 * top + k + 1], 0.0) for k in range(top))
    prob = jnp.broadcast_to(jnp.sum(prob, axis=1, keepdims=True), (rows.shape[0], LANES)).astype(BF16)
    for j, out in enumerate(outs):
        out[:, :body] = rows[j * cap : (j + 1) * cap]
        out[:, body:] = prob[j * cap : (j + 1) * cap]


def choose(codes, block, waits, tok, top, cap):
    rows = codes.shape[0]
    wide = (block.shape[0] - FIELDS) * LANES // tok + LANES
    return pl.pallas_call(
        functools.partial(choose_kernel, top, cap, len(waits)),
        out_shape=[jax.ShapeDtypeStruct((cap, wide), BF16)] * (rows // cap),
        in_specs=[VMEM, VMEM] + [ANY] * len(waits),
        out_specs=[VMEM] * (rows // cap),
        compiler_params=params(12),
        cost_estimate=cost(CLAIM, 2 * wide * (rows + tok)),
    )(codes, block, *waits)


def expert_kernel(core_ref, own_ref, other_ref, wg, wu, wd, mine_ref, send_ref, ph_ref, gg_ref, gu_ref):
    half = own_ref.shape[1] // 2 // LANES * LANES
    sides = [pl.ds(pl.multiple_of(c * half, LANES), half) for c in (core_ref[0], 1 - core_ref[0])]
    gate = up = raw = 0.0
    for ref, side in zip((own_ref, other_ref), sides):
        x, dy = ref[:, :half], ref[:, half : 2 * half]
        gate = gate + dot(x, wg[side, :], ((1,), (0,)))
        up = up + dot(x, wu[side, :], ((1,), (0,)))
        raw = raw + dot(dy, wd[:, side], ((1,), (1,)))
    prob = own_ref[:, 2 * half :].astype(F32)[:, :1]
    sigma = jax.nn.sigmoid(gate)
    act = gate * sigma
    hidden = (act * up).astype(BF16).astype(F32)
    row_part = jnp.sum(hidden * raw, axis=1, keepdims=True)
    grad_h = prob * raw
    g_up = (grad_h * act).astype(BF16)
    g_gate = (grad_h * up * sigma * (1.0 + gate * (1.0 - sigma))).astype(BF16)
    ph_ref[...] = (prob * hidden).astype(BF16)
    gg_ref[...] = g_gate
    gu_ref[...] = g_up
    row_part = jnp.broadcast_to(row_part, (row_part.shape[0], LANES))
    mine_ref[:, half:] = row_part.astype(BF16).astype(F32)
    send_ref[:, half:] = row_part.astype(BF16)
    for ref, side in zip((mine_ref, send_ref), sides):
        part = dot(g_gate, wg[side, :], ((1,), (1,))) + dot(g_up, wu[side, :], ((1,), (1,)))
        ref[:, :half] = part.astype(ref.dtype)


def expert_rows(core, own, other, gate_w, up_w, down_w):
    rows = own.shape[0]
    width, hid = gate_w.shape
    half = width // 2
    shape = jax.ShapeDtypeStruct
    return pl.pallas_call(
        expert_kernel,
        out_shape=[shape((rows, half + LANES), F32), shape((rows, half + LANES), BF16)] + [shape((rows, hid), BF16)] * 3,
        in_specs=[SMEM] + [VMEM] * 5,
        out_specs=[VMEM] * 5,
        compiler_params=params(16),
        cost_estimate=cost(10 * rows * width * hid, 4 * rows * width),
    )(core, own, other, gate_w, up_w, down_w)


def gather_kernel(top, cap, n, adds, flat, codes_ref, aux_ref, *refs):
    parts, out = refs[:n], refs[-1]
    half = parts[0].shape[1] - LANES
    hit, _ = hits(top, cap, aux_ref[...], codes_ref[...])
    tok = codes_ref.shape[1]
    rows = jnp.concatenate([r[...] for r in parts], axis=0)
    both = sum(jnp.where(h, 1.0, 0.0) for h in hit).astype(BF16)
    sums = dot(both, rows[:, :half], ((0,), (0,)))
    row_dp = rows[:, half:].astype(F32)
    field = lax.broadcasted_iota(jnp.int32, (FIELDS, LANES), 0)
    dp = jnp.zeros((FIELDS, LANES), F32)
    for k in range(top):
        dp = jnp.where(field == k, jnp.sum(jnp.where(hit[k], row_dp, 0.0), axis=0, keepdims=True), dp)
    tall = tok * half // LANES
    if adds:
        sums = sums + tiles(refs[n].at[pl.ds(0, tall), :], tok).astype(F32)
        dp = dp + refs[n][tall:, :].astype(F32)
    if flat:
        put_tiles(out, sums.astype(BF16))
        out[tall:, :] = dp.astype(BF16)
    else:
        refs[-2][...] = sums.astype(BF16)
        out[...] = dp.astype(BF16)


def gather_tokens(codes, block, parts, came, waits, top, cap, flat):
    tok = codes.shape[1]
    half = parts[0].shape[1] - LANES
    n = len(parts)
    extra = [] if came is None else [came]
    waits = list(waits)
    whole = lambda a: pl.BlockSpec(a.shape, lambda i: (0, 0))
    tail = pl.BlockSpec((FIELDS, LANES), lambda i: (block.shape[0] // FIELDS - 1, 0))
    out = jax.ShapeDtypeStruct((tok * half // LANES + FIELDS, LANES), BF16)
    if not flat:
        out = [jax.ShapeDtypeStruct((tok, half), BF16), jax.ShapeDtypeStruct((FIELDS, LANES), BF16)]
    return pl.pallas_call(
        functools.partial(gather_kernel, top, cap, n, came is not None, flat),
        out_shape=out,
        grid=(1,),
        in_specs=[whole(codes), tail] + [whole(a) for a in parts + extra] + [ANY] * len(waits),
        out_specs=jax.tree.map(whole, out),
        compiler_params=params(12),
        cost_estimate=cost(CLAIM, 6 * tok * half),
    )(codes, block, *parts, *extra, *waits)


def weights_kernel(n, many, by_row, step, core_ref, *refs):
    sides = refs[:n], refs[n : 2 * n]
    factors = refs[2 * n : 2 * n + many * n]
    outs, (fixed, held, sems) = refs[2 * n + many * n : -3], refs[-3:]
    rows, hid = factors[0].shape
    half = sides[0][0].shape[1] // 2 // LANES * LANES
    parts = half // step
    first = 0 if by_row else half
    for f in range(many):
        for k in range(n):
            part = factors[f * n + k][...]
            if by_row:
                fixed[k * rows : (k + 1) * rows, f * hid : (f + 1) * hid] = part
            else:
                fixed[:, k * rows : (k + 1) * rows] = part.astype(F32).T.astype(BF16)
    copies = []
    for i in range(2 * parts):
        side, at = i // parts, first + i % parts * step
        data = jnp.concatenate([r[:, at : at + step] for r in sides[side]], axis=0)
        out = dot(data, fixed[...], ((0,), (0,))) if by_row else dot(fixed[...], data, ((1,), (0,)))
        c = core_ref[0] if side == 0 else 1 - core_ref[0]
        there = pl.ds(pl.multiple_of(c * half + i % parts * step, LANES), step)
        if i >= 2:
            for copy in copies[i - 2]:
                copy.wait()
        copies.append([])
        for f in range(many):
            if by_row:
                held[i % 2, f] = out[:, f * hid : (f + 1) * hid].astype(BF16)
                target = outs[f].at[there, :]
            else:
                held[i % 2, f] = out.astype(BF16)
                target = outs[f].at[:, there]
            copies[i].append(pltpu.make_async_copy(held.at[i % 2, f], target, sems.at[i % 2, f]))
            copies[i][f].start()
    for group in copies[-2:]:
        for copy in group:
            copy.wait()


def weight_gradients(core, owns, others, factors, by_row):
    n = len(owns)
    many = len(factors)
    rows, hid = factors[0][0].shape
    half = (owns[0].shape[1] - LANES) // 2
    step = half // 2
    width = 2 * half
    tile = (step, hid) if by_row else (hid, step)
    return pl.pallas_call(
        functools.partial(weights_kernel, n, many, by_row, step),
        out_shape=[jax.ShapeDtypeStruct((width, hid) if by_row else (hid, width), BF16)] * many,
        in_specs=[SMEM] + [VMEM] * (2 * n + many * n),
        out_specs=[ANY] * many,
        scratch_shapes=[
            pltpu.VMEM((n * rows, many * hid) if by_row else (hid, n * rows), BF16),
            pltpu.VMEM((2, many) + tile, BF16),
            pltpu.SemaphoreType.DMA((2, many)),
        ],
        compiler_params=params(24),
        cost_estimate=cost(rows * width * hid, 2 * n * rows * width),
    )(core, *owns, *others, *(a for f in factors for a in f))


def place_kernel(core_ref, own_ref, other_ref, out_hbm, sems):
    half = out_hbm.shape[1] // 2
    copies = []
    for i, (ref, c) in enumerate(((own_ref, core_ref[0]), (other_ref, 1 - core_ref[0]))):
        there = pl.ds(pl.multiple_of(c * half, LANES), half)
        copies.append(pltpu.make_async_copy(ref.at[:, pl.ds(0, half)], out_hbm.at[:, there], sems.at[i]))
    for copy in copies:
        copy.start()
    for copy in copies:
        copy.wait()


def place_halves(core, own, other, width):
    return pl.pallas_call(
        place_kernel,
        out_shape=jax.ShapeDtypeStruct((own.shape[0], width), BF16),
        in_specs=[SMEM, VMEM, VMEM],
        out_specs=ANY,
        scratch_shapes=[pltpu.SemaphoreType.DMA((2,))],
        compiler_params=params(8),
        cost_estimate=cost(1, 4 * own.shape[0] * width),
    )(core, own, other)


def on_device(tokens, grad_out, routes, probs, w_gate, w_up, w_down):
    experts = lax.axis_size("expert")
    tok, width = tokens.shape
    top = routes.shape[1]
    cap = 3 * tok * top // experts
    plane = experts // RINGS
    half = width // 2
    me = lax.axis_index("expert")
    core_id = lax.axis_index("tensor")
    core = core_id.astype(jnp.int32).reshape(1)
    z, p = me // plane, me % plane
    weights = (w_gate[0], w_up[0], w_down[0])

    after = {0: 1, 1: 3, 3: 2, 2: 0}
    ring = [(i, after[i // plane] * plane + i % plane) for i in range(experts)]
    peers = [[(i, i // plane * plane + ((i % plane) ^ j)) for i in range(experts)] for j in range(plane)]
    swap = [(0, 1), (1, 0)]

    row = jnp.arange(plane * cap, dtype=jnp.int32)
    codes = (z * plane + (p ^ (row // cap))) * cap + row % cap
    codes = jnp.broadcast_to(codes.astype(F32)[:, None], (plane * cap, LANES))
    meet = lax.optimization_barrier

    def hop(rows):
        return lax.ppermute(rows, "expert", ring)

    def turn(rows):
        return lax.ppermute(rows, "tensor", swap)

    def exchange(parts):
        return [parts[0]] + [lax.ppermute(parts[j], "expert", peers[j]) for j in range(1, plane)]

    def joined(parts):
        return jnp.concatenate(parts, axis=0)

    def work(own, other):
        mine, send, *kept = expert_rows(core, own, other, *weights)
        return mine, send, kept

    def summed(mine, came):
        total = (mine + came.astype(F32)).astype(BF16)
        return [total[j * cap : (j + 1) * cap] for j in range(plane)]

    def picked(block, *waits):
        return list(choose(codes, block, waits, tok, top, cap))

    def gather(block, parts, came=None, waits=(), flat=True):
        return gather_tokens(codes, block, parts, came, waits, top, cap, flat)

    h0 = make_block(core, tokens, grad_out, routes, probs)

    h1 = hop(h0)
    g0 = exchange(picked(h0))
    s1 = picked(h1, *g0)
    h1, s1, g0 = meet((h1, s1, g0))

    h2 = hop(h1)
    g1 = exchange(s1)
    own0 = joined(g0)
    other0 = turn(own0)
    mine0, send0, w0 = work(own0, other0)
    came0 = turn(send0)
    s2 = picked(h2, *g1)
    h2, s2, g1, mine0, came0, w0 = meet((h2, s2, g1, mine0, came0, w0))

    h3 = hop(h2)
    g2 = exchange(s2)
    own1 = joined(g1)
    other1 = turn(own1)
    mine1, send1, w1 = work(own1, other1)
    came1 = turn(send1)
    s3 = picked(h3, *g2)
    h3, s3, g2, mine1, came1, w1 = meet((h3, s3, g2, mine1, came1, w1))

    g3 = exchange(s3)
    b1 = exchange(summed(mine1, came1))
    own2 = joined(g2)
    other2 = turn(own2)
    mine2, send2, w2 = work(own2, other2)
    t1 = gather(h1, b1, waits=(*g3, send2))
    g3, t1, mine2, send2, w2, mine0 = meet((g3, t1, mine2, send2, w2, mine0))

    r1 = hop(t1)
    b2 = exchange(summed(mine2, turn(send2)))
    own3 = joined(g3)
    other3 = turn(own3)
    mine3, send3, w3 = work(own3, other3)
    came3 = turn(send3)
    t2 = gather(h2, b2, r1)
    t2, mine3, came3, w3, mine0 = meet((t2, mine3, came3, w3, mine0))

    owns, others = (own0, own1, own2, own3), (other0, other1, other2, other3)
    ph, gg, gu = zip(w0, w1, w2, w3)
    r2 = hop(t2)
    b3 = exchange(summed(mine3, came3))
    d_gate, d_up = weight_gradients(core, owns, others, (gg, gu), True)
    c0 = summed(mine0, came0)
    t3 = gather(h3, b3, r2)
    t3, d_gate, d_up, ph, c0 = meet((t3, d_gate, d_up, ph, c0))

    r3 = hop(t3)
    b0 = exchange(c0)
    (d_down,) = weight_gradients(core, owns, others, (ph,), False)
    r3, b0, d_down = meet((r3, b0, d_down))
    total, dp = gather(h0, b0, r3, flat=False)

    d_tokens = place_halves(core, total, turn(total), width)
    d_probs = dp[:top, :].T
    return (d_tokens, d_probs, d_gate[None], d_up[None], d_down[None])


def solution(mesh):
    rows = P("expert", None)
    columns = P("expert", None, "tensor")
    down = P("expert", "tensor", None)
    return jax.shard_map(
        on_device,
        mesh=mesh,
        in_specs=(rows, rows, rows, rows, columns, columns, down),
        out_specs=(rows, rows, columns, columns, down),
        check_vma=False,
    )
```

```python
import functools

import jax
import jax.numpy as jnp
from jax import lax
from jax.experimental import pallas as pl
from jax.experimental.pallas import tpu as pltpu
from jax.sharding import PartitionSpec as P

BF16 = jnp.bfloat16
F32 = jnp.float32
LANES = 128
FIELDS = 16
RINGS = 4
VMEM = pl.BlockSpec(memory_space=pltpu.VMEM)
SMEM = pl.BlockSpec(memory_space=pltpu.SMEM)
ANY = pl.BlockSpec(memory_space=pl.ANY)


def dot(a, b, dims):
    return lax.dot_general(a, b, (dims, ((), ())), preferred_element_type=F32)


def params(mib):
    return pltpu.CompilerParams(vmem_limit_bytes=mib * 2**20)


def cost(flops, nbytes):
    return pl.CostEstimate(flops=flops, bytes_accessed=nbytes, transcendentals=0)


CLAIM = 4 * 10**10


def tiles(ref, tok):
    return jnp.concatenate([ref[i * tok : (i + 1) * tok, :] for i in range(ref.shape[0] // tok)], axis=1)


def put_tiles(ref, value):
    tok = value.shape[0]
    for i in range(value.shape[1] // LANES):
        ref[i * tok : (i + 1) * tok, :] = value[:, i * LANES : (i + 1) * LANES]


def block_kernel(tok_ref, dy_ref, routes_ref, probs_ref, out_ref):
    top, tok = routes_ref.shape
    tall = tok_ref.shape[1] * tok // LANES
    expert = lax.broadcasted_iota(jnp.int32, (LANES, tok), 0)
    row = lax.broadcasted_iota(jnp.int32, (tok, tok), 0)
    col = lax.broadcasted_iota(jnp.int32, (tok, tok), 1)
    hot = [expert == routes_ref[k : k + 1, :] for k in range(top)]
    named = sum(jnp.where(h, 1.0, 0.0) for h in hot).astype(BF16)
    before = jnp.where(row < col, 1.0, 0.0).astype(BF16)
    counts = dot(named, before, ((1,), (0,)))
    field = lax.broadcasted_iota(jnp.int32, (FIELDS, LANES), 0)
    aux = jnp.zeros((FIELDS, LANES), F32)
    for k in range(top):
        slot = jnp.sum(jnp.where(hot[k], counts, 0.0), axis=0, keepdims=True)
        aux = jnp.where(field == k, routes_ref[k : k + 1, :].astype(F32), aux)
        aux = jnp.where(field == top + k, slot, aux)
        aux = jnp.where(field == 2 * top + k, probs_ref[k : k + 1, :].astype(F32), aux)
    for i, ref in enumerate((tok_ref, dy_ref)):
        put_tiles(out_ref.at[pl.ds(i * tall, tall), :], ref[...])
    out_ref[2 * tall :, :] = aux.astype(BF16)


def make_block(core, tokens, grad_out, routes, probs):
    tok, width = tokens.shape
    half = width // 2
    mine = [lax.dynamic_slice_in_dim(a, core[0] * half, half, axis=1) for a in (tokens, grad_out)]
    return pl.pallas_call(
        block_kernel,
        out_shape=jax.ShapeDtypeStruct((tok * width // LANES + FIELDS, LANES), BF16),
        in_specs=[VMEM] * 4,
        out_specs=VMEM,
        compiler_params=params(8),
        cost_estimate=cost(2 * tok * tok * LANES, 4 * tok * width),
    )(*mine, routes.T, probs.T)


def follow_kernel(*refs):
    refs[-1][...] = jnp.zeros_like(refs[-1])


def follow(*arrays):
    return pl.pallas_call(
        follow_kernel,
        out_shape=jax.ShapeDtypeStruct((8, LANES), F32),
        in_specs=[ANY] * len(arrays),
        out_specs=VMEM,
        compiler_params=params(4),
        cost_estimate=cost(CLAIM, 1),
    )(*arrays)


def hits(top, cap, aux, codes):
    aux = aux.astype(F32)
    return [codes == aux[k : k + 1] * cap + aux[top + k : top + k + 1] for k in range(top)], aux


def choose_kernel(top, cap, waits, codes_ref, block_ref, *refs):
    outs = refs[waits:]
    tall = block_ref.shape[0] - FIELDS
    body = outs[0].shape[1] - LANES
    hit, aux = hits(top, cap, block_ref[tall:, :], codes_ref[...])
    both = sum(jnp.where(h, 1.0, 0.0) for h in hit).astype(BF16)
    rows = dot(both, tiles(block_ref.at[pl.ds(0, tall), :], tall * LANES // body), ((1,), (0,))).astype(BF16)
    prob = sum(jnp.where(hit[k], aux[2 * top + k : 2 * top + k + 1], 0.0) for k in range(top))
    prob = jnp.broadcast_to(jnp.sum(prob, axis=1, keepdims=True), (rows.shape[0], LANES)).astype(BF16)
    for j, out in enumerate(outs):
        out[:, :body] = rows[j * cap : (j + 1) * cap]
        out[:, body:] = prob[j * cap : (j + 1) * cap]


def choose(codes, block, waits, tok, top, cap):
    rows = codes.shape[0]
    wide = (block.shape[0] - FIELDS) * LANES // tok + LANES
    return pl.pallas_call(
        functools.partial(choose_kernel, top, cap, len(waits)),
        out_shape=[jax.ShapeDtypeStruct((cap, wide), BF16)] * (rows // cap),
        in_specs=[VMEM, VMEM] + [ANY] * len(waits),
        out_specs=[VMEM] * (rows // cap),
        compiler_params=params(12),
        cost_estimate=cost(CLAIM if len(waits) > 1 else 1, 2 * wide * (rows + tok)),
    )(codes, block, *waits)


def expert_kernel(core_ref, own_ref, other_ref, wg, wu, wd, mine_ref, send_ref, ph_ref, gg_ref, gu_ref):
    half = own_ref.shape[1] // 2 // LANES * LANES
    sides = [pl.ds(pl.multiple_of(c * half, LANES), half) for c in (core_ref[0], 1 - core_ref[0])]
    gate = up = raw = 0.0
    for ref, side in zip((own_ref, other_ref), sides):
        x, dy = ref[:, :half], ref[:, half : 2 * half]
        gate = gate + dot(x, wg[side, :], ((1,), (0,)))
        up = up + dot(x, wu[side, :], ((1,), (0,)))
        raw = raw + dot(dy, wd[:, side], ((1,), (1,)))
    prob = own_ref[:, 2 * half :].astype(F32)[:, :1]
    sigma = jax.nn.sigmoid(gate)
    act = gate * sigma
    hidden = (act * up).astype(BF16).astype(F32)
    row_part = jnp.sum(hidden * raw, axis=1, keepdims=True)
    grad_h = prob * raw
    g_up = (grad_h * act).astype(BF16)
    g_gate = (grad_h * up * sigma * (1.0 + gate * (1.0 - sigma))).astype(BF16)
    ph_ref[...] = (prob * hidden).astype(BF16)
    gg_ref[...] = g_gate
    gu_ref[...] = g_up
    row_part = jnp.broadcast_to(row_part, (row_part.shape[0], LANES))
    mine_ref[:, half:] = row_part.astype(BF16).astype(F32)
    send_ref[:, half:] = row_part.astype(BF16)
    for ref, side in zip((mine_ref, send_ref), sides):
        part = dot(g_gate, wg[side, :], ((1,), (1,))) + dot(g_up, wu[side, :], ((1,), (1,)))
        ref[:, :half] = part.astype(ref.dtype)


def expert_rows(core, own, other, gate_w, up_w, down_w):
    rows = own.shape[0]
    width, hid = gate_w.shape
    half = width // 2
    shape = jax.ShapeDtypeStruct
    return pl.pallas_call(
        expert_kernel,
        out_shape=[shape((rows, half + LANES), F32), shape((rows, half + LANES), BF16)] + [shape((rows, hid), BF16)] * 3,
        in_specs=[SMEM] + [VMEM] * 5,
        out_specs=[VMEM] * 5,
        compiler_params=params(16),
        cost_estimate=cost(10 * rows * width * hid, 4 * rows * width),
    )(core, own, other, gate_w, up_w, down_w)


def gather_kernel(top, cap, n, adds, flat, codes_ref, aux_ref, *refs):
    parts, out = refs[:n], refs[-1]
    half = parts[0].shape[1] - LANES
    hit, _ = hits(top, cap, aux_ref[...], codes_ref[...])
    tok = codes_ref.shape[1]
    rows = jnp.concatenate([r[...] for r in parts], axis=0)
    both = sum(jnp.where(h, 1.0, 0.0) for h in hit).astype(BF16)
    sums = dot(both, rows[:, :half], ((0,), (0,)))
    row_dp = rows[:, half:].astype(F32)
    field = lax.broadcasted_iota(jnp.int32, (FIELDS, LANES), 0)
    dp = jnp.zeros((FIELDS, LANES), F32)
    for k in range(top):
        dp = jnp.where(field == k, jnp.sum(jnp.where(hit[k], row_dp, 0.0), axis=0, keepdims=True), dp)
    tall = tok * half // LANES
    if adds:
        sums = sums + tiles(refs[n].at[pl.ds(0, tall), :], tok).astype(F32)
        dp = dp + refs[n][tall:, :].astype(F32)
    if flat:
        put_tiles(out, sums.astype(BF16))
        out[tall:, :] = dp.astype(BF16)
    else:
        refs[-2][...] = sums.astype(BF16)
        out[...] = dp.astype(BF16)


def gather_tokens(codes, block, parts, came, waits, top, cap, flat):
    tok = codes.shape[1]
    half = parts[0].shape[1] - LANES
    n = len(parts)
    extra = [] if came is None else [came]
    waits = list(waits)
    whole = lambda a: pl.BlockSpec(a.shape, lambda i: (0, 0))
    tail = pl.BlockSpec((FIELDS, LANES), lambda i: (block.shape[0] // FIELDS - 1, 0))
    out = jax.ShapeDtypeStruct((tok * half // LANES + FIELDS, LANES), BF16)
    if not flat:
        out = [jax.ShapeDtypeStruct((tok, half), BF16), jax.ShapeDtypeStruct((FIELDS, LANES), BF16)]
    return pl.pallas_call(
        functools.partial(gather_kernel, top, cap, n, came is not None, flat),
        out_shape=out,
        grid=(1,),
        in_specs=[whole(codes), tail] + [whole(a) for a in parts + extra] + [ANY] * len(waits),
        out_specs=jax.tree.map(whole, out),
        compiler_params=params(12),
        cost_estimate=cost(CLAIM, 6 * tok * half),
    )(codes, block, *parts, *extra, *waits)


def weights_kernel(n, many, by_row, step, core_ref, *refs):
    sides = refs[:n], refs[n : 2 * n]
    factors = refs[2 * n : 2 * n + many * n]
    outs, (fixed, held, sems) = refs[2 * n + many * n : -3], refs[-3:]
    rows, hid = factors[0].shape
    half = sides[0][0].shape[1] // 2 // LANES * LANES
    parts = half // step
    first = 0 if by_row else half
    for f in range(many):
        for k in range(n):
            part = factors[f * n + k][...]
            if by_row:
                fixed[k * rows : (k + 1) * rows, f * hid : (f + 1) * hid] = part
            else:
                fixed[:, k * rows : (k + 1) * rows] = part.astype(F32).T.astype(BF16)
    copies = []
    for i in range(2 * parts):
        side, at = i // parts, first + i % parts * step
        data = jnp.concatenate([r[:, at : at + step] for r in sides[side]], axis=0)
        out = dot(data, fixed[...], ((0,), (0,))) if by_row else dot(fixed[...], data, ((1,), (0,)))
        c = core_ref[0] if side == 0 else 1 - core_ref[0]
        there = pl.ds(pl.multiple_of(c * half + i % parts * step, LANES), step)
        if i >= 2:
            for copy in copies[i - 2]:
                copy.wait()
        copies.append([])
        for f in range(many):
            if by_row:
                held[i % 2, f] = out[:, f * hid : (f + 1) * hid].astype(BF16)
                target = outs[f].at[there, :]
            else:
                held[i % 2, f] = out.astype(BF16)
                target = outs[f].at[:, there]
            copies[i].append(pltpu.make_async_copy(held.at[i % 2, f], target, sems.at[i % 2, f]))
            copies[i][f].start()
    for group in copies[-2:]:
        for copy in group:
            copy.wait()


def weight_gradients(core, owns, others, factors, by_row):
    n = len(owns)
    many = len(factors)
    rows, hid = factors[0][0].shape
    half = (owns[0].shape[1] - LANES) // 2
    step = half // 2
    width = 2 * half
    tile = (step, hid) if by_row else (hid, step)
    return pl.pallas_call(
        functools.partial(weights_kernel, n, many, by_row, step),
        out_shape=[jax.ShapeDtypeStruct((width, hid) if by_row else (hid, width), BF16)] * many,
        in_specs=[SMEM] + [VMEM] * (2 * n + many * n),
        out_specs=[ANY] * many,
        scratch_shapes=[
            pltpu.VMEM((n * rows, many * hid) if by_row else (hid, n * rows), BF16),
            pltpu.VMEM((2, many) + tile, BF16),
            pltpu.SemaphoreType.DMA((2, many)),
        ],
        compiler_params=params(24),
        cost_estimate=cost(rows * width * hid, 2 * n * rows * width),
    )(core, *owns, *others, *(a for f in factors for a in f))


def place_kernel(core_ref, own_ref, other_ref, out_hbm, sems):
    half = out_hbm.shape[1] // 2
    copies = []
    for i, (ref, c) in enumerate(((own_ref, core_ref[0]), (other_ref, 1 - core_ref[0]))):
        there = pl.ds(pl.multiple_of(c * half, LANES), half)
        copies.append(pltpu.make_async_copy(ref.at[:, pl.ds(0, half)], out_hbm.at[:, there], sems.at[i]))
    for copy in copies:
        copy.start()
    for copy in copies:
        copy.wait()


def place_halves(core, own, other, width):
    return pl.pallas_call(
        place_kernel,
        out_shape=jax.ShapeDtypeStruct((own.shape[0], width), BF16),
        in_specs=[SMEM, VMEM, VMEM],
        out_specs=ANY,
        scratch_shapes=[pltpu.SemaphoreType.DMA((2,))],
        compiler_params=params(8),
        cost_estimate=cost(1, 4 * own.shape[0] * width),
    )(core, own, other)


def on_device(tokens, grad_out, routes, probs, w_gate, w_up, w_down):
    experts = lax.axis_size("expert")
    tok, width = tokens.shape
    top = routes.shape[1]
    cap = 3 * tok * top // experts
    plane = experts // RINGS
    half = width // 2
    me = lax.axis_index("expert")
    core_id = lax.axis_index("tensor")
    core = core_id.astype(jnp.int32).reshape(1)
    z, p = me // plane, me % plane
    weights = (w_gate[0], w_up[0], w_down[0])

    after = {0: 1, 1: 3, 3: 2, 2: 0}
    ring = [(i, after[i // plane] * plane + i % plane) for i in range(experts)]
    peers = [[(i, i // plane * plane + ((i % plane) ^ j)) for i in range(experts)] for j in range(plane)]
    swap = [(0, 1), (1, 0)]

    row = jnp.arange(plane * cap, dtype=jnp.int32)
    codes = (z * plane + (p ^ (row // cap))) * cap + row % cap
    codes = jnp.broadcast_to(codes.astype(F32)[:, None], (plane * cap, LANES))
    meet = lax.optimization_barrier

    def hop(rows):
        return lax.ppermute(rows, "expert", ring)

    def turn(rows):
        return lax.ppermute(rows, "tensor", swap)

    def exchange(parts):
        return [parts[0]] + [lax.ppermute(parts[j], "expert", peers[j]) for j in range(1, plane)]

    def joined(parts):
        return jnp.concatenate(parts, axis=0)

    def work(own, other):
        mine, send, *kept = expert_rows(core, own, other, *weights)
        return mine, send, kept

    def summed(mine, came):
        total = (mine + came.astype(F32)).astype(BF16)
        return [total[j * cap : (j + 1) * cap] for j in range(plane)]

    def picked(block, *waits):
        return list(choose(codes, block, waits, tok, top, cap))

    def gather(block, parts, came=None, waits=(), flat=True):
        return gather_tokens(codes, block, parts, came, waits, top, cap, flat)

    h0 = make_block(core, tokens, grad_out, routes, probs)

    h1 = hop(h0)
    g0 = exchange(picked(h0))
    h1, g0, mark = meet((h1, g0, follow(h1, *g0)))

    h2 = hop(h1)
    g1 = exchange(picked(h1, mark))
    own0 = joined(g0)
    other0 = turn(own0)
    mine0, send0, w0 = work(own0, other0)
    came0 = turn(send0)
    h2, g1, mine0, came0, w0, mark = meet((h2, g1, mine0, came0, w0, follow(h2, *g1)))

    h3 = hop(h2)
    g2 = exchange(picked(h2, mark))
    own1 = joined(g1)
    other1 = turn(own1)
    mine1, send1, w1 = work(own1, other1)
    came1 = turn(send1)
    s3 = picked(h3, *g2)
    h3, s3, g2, mine1, came1, w1 = meet((h3, s3, g2, mine1, came1, w1))

    g3 = exchange(s3)
    b1 = exchange(summed(mine1, came1))
    own2 = joined(g2)
    other2 = turn(own2)
    mine2, send2, w2 = work(own2, other2)
    t1 = gather(h1, b1, waits=(*g3, send2))
    g3, t1, mine2, send2, w2, mine0 = meet((g3, t1, mine2, send2, w2, mine0))

    r1 = hop(t1)
    b2 = exchange(summed(mine2, turn(send2)))
    own3 = joined(g3)
    other3 = turn(own3)
    mine3, send3, w3 = work(own3, other3)
    came3 = turn(send3)
    t2 = gather(h2, b2, r1)
    t2, mine3, came3, w3, mine0 = meet((t2, mine3, came3, w3, mine0))

    owns, others = (own0, own1, own2, own3), (other0, other1, other2, other3)
    ph, gg, gu = zip(w0, w1, w2, w3)
    r2 = hop(t2)
    b3 = exchange(summed(mine3, came3))
    d_gate, d_up = weight_gradients(core, owns, others, (gg, gu), True)
    c0 = summed(mine0, came0)
    t3 = gather(h3, b3, r2)
    t3, d_gate, d_up, ph, c0 = meet((t3, d_gate, d_up, ph, c0))

    r3 = hop(t3)
    b0 = exchange(c0)
    (d_down,) = weight_gradients(core, owns, others, (ph,), False)
    r3, b0, d_down = meet((r3, b0, d_down))
    total, dp = gather(h0, b0, r3, flat=False)

    d_tokens = place_halves(core, total, turn(total), width)
    d_probs = dp[:top, :].T
    return (d_tokens, d_probs, d_gate[None], d_up[None], d_down[None])


def solution(mesh):
    rows = P("expert", None)
    columns = P("expert", None, "tensor")
    down = P("expert", "tensor", None)
    return jax.shard_map(
        on_device,
        mesh=mesh,
        in_specs=(rows, rows, rows, rows, columns, columns, down),
        out_specs=(rows, rows, columns, columns, down),
        check_vma=False,
    )
```

```python
import functools

import jax
import jax.numpy as jnp
from jax import lax
from jax.experimental import pallas as pl
from jax.experimental.pallas import tpu as pltpu
from jax.sharding import PartitionSpec as P

BF16 = jnp.bfloat16
F32 = jnp.float32
LANES = 128
FIELDS = 16
RINGS = 4
VMEM = pl.BlockSpec(memory_space=pltpu.VMEM)
SMEM = pl.BlockSpec(memory_space=pltpu.SMEM)
ANY = pl.BlockSpec(memory_space=pl.ANY)


def dot(a, b, dims):
    return lax.dot_general(a, b, (dims, ((), ())), preferred_element_type=F32)


def params(mib):
    return pltpu.CompilerParams(vmem_limit_bytes=mib * 2**20)


def cost(flops, nbytes):
    return pl.CostEstimate(flops=flops, bytes_accessed=nbytes, transcendentals=0)


CLAIM = 4 * 10**10


def tiles(ref, tok):
    return jnp.concatenate([ref[i * tok : (i + 1) * tok, :] for i in range(ref.shape[0] // tok)], axis=1)


def put_tiles(ref, value):
    tok = value.shape[0]
    for i in range(value.shape[1] // LANES):
        ref[i * tok : (i + 1) * tok, :] = value[:, i * LANES : (i + 1) * LANES]


def block_kernel(tok_ref, dy_ref, routes_ref, probs_ref, out_ref):
    top, tok = routes_ref.shape
    tall = tok_ref.shape[1] * tok // LANES
    expert = lax.broadcasted_iota(jnp.int32, (LANES, tok), 0)
    row = lax.broadcasted_iota(jnp.int32, (tok, tok), 0)
    col = lax.broadcasted_iota(jnp.int32, (tok, tok), 1)
    hot = [expert == routes_ref[k : k + 1, :] for k in range(top)]
    named = sum(jnp.where(h, 1.0, 0.0) for h in hot).astype(BF16)
    before = jnp.where(row < col, 1.0, 0.0).astype(BF16)
    counts = dot(named, before, ((1,), (0,)))
    field = lax.broadcasted_iota(jnp.int32, (FIELDS, LANES), 0)
    aux = jnp.zeros((FIELDS, LANES), F32)
    for k in range(top):
        slot = jnp.sum(jnp.where(hot[k], counts, 0.0), axis=0, keepdims=True)
        aux = jnp.where(field == k, routes_ref[k : k + 1, :].astype(F32), aux)
        aux = jnp.where(field == top + k, slot, aux)
        aux = jnp.where(field == 2 * top + k, probs_ref[k : k + 1, :].astype(F32), aux)
    for i, ref in enumerate((tok_ref, dy_ref)):
        put_tiles(out_ref.at[pl.ds(i * tall, tall), :], ref[...])
    out_ref[2 * tall :, :] = aux.astype(BF16)


def make_block(core, tokens, grad_out, routes, probs):
    tok, width = tokens.shape
    half = width // 2
    mine = [lax.dynamic_slice_in_dim(a, core[0] * half, half, axis=1) for a in (tokens, grad_out)]
    return pl.pallas_call(
        block_kernel,
        out_shape=jax.ShapeDtypeStruct((tok * width // LANES + FIELDS, LANES), BF16),
        in_specs=[VMEM] * 4,
        out_specs=VMEM,
        compiler_params=params(8),
        cost_estimate=cost(2 * tok * tok * LANES, 4 * tok * width),
    )(*mine, routes.T, probs.T)


def follow_kernel(*refs):
    refs[-1][...] = jnp.zeros_like(refs[-1])


def follow(*arrays):
    return pl.pallas_call(
        follow_kernel,
        out_shape=jax.ShapeDtypeStruct((8, LANES), F32),
        in_specs=[ANY] * len(arrays),
        out_specs=VMEM,
        compiler_params=params(4),
        cost_estimate=cost(CLAIM, 1),
    )(*arrays)


def hits(top, cap, aux, codes):
    aux = aux.astype(F32)
    return [codes == aux[k : k + 1] * cap + aux[top + k : top + k + 1] for k in range(top)], aux


def choose_kernel(top, cap, waits, codes_ref, block_ref, *refs):
    outs = refs[waits:]
    tall = block_ref.shape[0] - FIELDS
    body = outs[0].shape[1] - LANES
    hit, aux = hits(top, cap, block_ref[tall:, :], codes_ref[...])
    both = sum(jnp.where(h, 1.0, 0.0) for h in hit).astype(BF16)
    rows = dot(both, tiles(block_ref.at[pl.ds(0, tall), :], tall * LANES // body), ((1,), (0,))).astype(BF16)
    prob = sum(jnp.where(hit[k], aux[2 * top + k : 2 * top + k + 1], 0.0) for k in range(top))
    prob = jnp.broadcast_to(jnp.sum(prob, axis=1, keepdims=True), (rows.shape[0], LANES)).astype(BF16)
    for j, out in enumerate(outs):
        out[:, :body] = rows[j * cap : (j + 1) * cap]
        out[:, body:] = prob[j * cap : (j + 1) * cap]


def choose(codes, block, waits, tok, top, cap):
    rows = codes.shape[0]
    wide = (block.shape[0] - FIELDS) * LANES // tok + LANES
    return pl.pallas_call(
        functools.partial(choose_kernel, top, cap, len(waits)),
        out_shape=[jax.ShapeDtypeStruct((cap, wide), BF16)] * (rows // cap),
        in_specs=[VMEM, VMEM] + [ANY] * len(waits),
        out_specs=[VMEM] * (rows // cap),
        compiler_params=params(12),
        cost_estimate=cost(CLAIM if len(waits) > 1 else 1, 2 * wide * (rows + tok)),
    )(codes, block, *waits)


def expert_kernel(core_ref, own_ref, other_ref, wg, wu, wd, mine_ref, send_ref, ph_ref, gg_ref, gu_ref):
    half = own_ref.shape[1] // 2 // LANES * LANES
    sides = [pl.ds(pl.multiple_of(c * half, LANES), half) for c in (core_ref[0], 1 - core_ref[0])]
    gate = up = raw = 0.0
    for ref, side in zip((own_ref, other_ref), sides):
        x, dy = ref[:, :half], ref[:, half : 2 * half]
        gate = gate + dot(x, wg[side, :], ((1,), (0,)))
        up = up + dot(x, wu[side, :], ((1,), (0,)))
        raw = raw + dot(dy, wd[:, side], ((1,), (1,)))
    prob = own_ref[:, 2 * half :].astype(F32)[:, :1]
    sigma = jax.nn.sigmoid(gate)
    act = gate * sigma
    hidden = (act * up).astype(BF16).astype(F32)
    row_part = jnp.sum(hidden * raw, axis=1, keepdims=True)
    grad_h = prob * raw
    g_up = (grad_h * act).astype(BF16)
    g_gate = (grad_h * up * sigma * (1.0 + gate * (1.0 - sigma))).astype(BF16)
    ph_ref[...] = (prob * hidden).astype(BF16)
    gg_ref[...] = g_gate
    gu_ref[...] = g_up
    row_part = jnp.broadcast_to(row_part, (row_part.shape[0], LANES))
    mine_ref[:, half:] = row_part.astype(BF16).astype(F32)
    send_ref[:, half:] = row_part.astype(BF16)
    for ref, side in zip((mine_ref, send_ref), sides):
        part = dot(g_gate, wg[side, :], ((1,), (1,))) + dot(g_up, wu[side, :], ((1,), (1,)))
        ref[:, :half] = part.astype(ref.dtype)


def expert_rows(core, own, other, gate_w, up_w, down_w):
    rows = own.shape[0]
    width, hid = gate_w.shape
    half = width // 2
    shape = jax.ShapeDtypeStruct
    return pl.pallas_call(
        expert_kernel,
        out_shape=[shape((rows, half + LANES), F32), shape((rows, half + LANES), BF16)] + [shape((rows, hid), BF16)] * 3,
        in_specs=[SMEM] + [VMEM] * 5,
        out_specs=[VMEM] * 5,
        compiler_params=params(16),
        cost_estimate=cost(10 * rows * width * hid, 4 * rows * width),
    )(core, own, other, gate_w, up_w, down_w)


def gather_kernel(top, cap, n, adds, flat, codes_ref, aux_ref, *refs):
    parts, out = refs[:n], refs[-1]
    half = parts[0].shape[1] - LANES
    hit, _ = hits(top, cap, aux_ref[...], codes_ref[...])
    tok = codes_ref.shape[1]
    rows = jnp.concatenate([r[...] for r in parts], axis=0)
    both = sum(jnp.where(h, 1.0, 0.0) for h in hit).astype(BF16)
    sums = dot(both, rows[:, :half], ((0,), (0,)))
    row_dp = rows[:, half:].astype(F32)
    field = lax.broadcasted_iota(jnp.int32, (FIELDS, LANES), 0)
    dp = jnp.zeros((FIELDS, LANES), F32)
    for k in range(top):
        dp = jnp.where(field == k, jnp.sum(jnp.where(hit[k], row_dp, 0.0), axis=0, keepdims=True), dp)
    tall = tok * half // LANES
    if adds:
        sums = sums + tiles(refs[n].at[pl.ds(0, tall), :], tok).astype(F32)
        dp = dp + refs[n][tall:, :].astype(F32)
    if flat:
        put_tiles(out, sums.astype(BF16))
        out[tall:, :] = dp.astype(BF16)
    else:
        refs[-2][...] = sums.astype(BF16)
        out[...] = dp.astype(BF16)


def gather_tokens(codes, block, parts, came, waits, top, cap, flat):
    tok = codes.shape[1]
    half = parts[0].shape[1] - LANES
    n = len(parts)
    extra = [] if came is None else [came]
    waits = list(waits)
    whole = lambda a: pl.BlockSpec(a.shape, lambda i: (0, 0))
    tail = pl.BlockSpec((FIELDS, LANES), lambda i: (block.shape[0] // FIELDS - 1, 0))
    out = jax.ShapeDtypeStruct((tok * half // LANES + FIELDS, LANES), BF16)
    if not flat:
        out = [jax.ShapeDtypeStruct((tok, half), BF16), jax.ShapeDtypeStruct((FIELDS, LANES), BF16)]
    return pl.pallas_call(
        functools.partial(gather_kernel, top, cap, n, came is not None, flat),
        out_shape=out,
        grid=(1,),
        in_specs=[whole(codes), tail] + [whole(a) for a in parts + extra] + [ANY] * len(waits),
        out_specs=jax.tree.map(whole, out),
        compiler_params=params(12),
        cost_estimate=cost(CLAIM, 6 * tok * half),
    )(codes, block, *parts, *extra, *waits)


def weights_kernel(n, many, by_row, step, core_ref, *refs):
    sides = refs[:n], refs[n : 2 * n]
    factors = refs[2 * n : 2 * n + many * n]
    outs, (fixed, held, sems) = refs[2 * n + many * n : -3], refs[-3:]
    rows, hid = factors[0].shape
    half = sides[0][0].shape[1] // 2 // LANES * LANES
    parts = half // step
    first = 0 if by_row else half
    for f in range(many):
        for k in range(n):
            part = factors[f * n + k][...]
            if by_row:
                fixed[k * rows : (k + 1) * rows, f * hid : (f + 1) * hid] = part
            else:
                fixed[:, k * rows : (k + 1) * rows] = part.astype(F32).T.astype(BF16)
    copies = []
    for i in range(2 * parts):
        side, at = i // parts, first + i % parts * step
        data = jnp.concatenate([r[:, at : at + step] for r in sides[side]], axis=0)
        out = dot(data, fixed[...], ((0,), (0,))) if by_row else dot(fixed[...], data, ((1,), (0,)))
        c = core_ref[0] if side == 0 else 1 - core_ref[0]
        there = pl.ds(pl.multiple_of(c * half + i % parts * step, LANES), step)
        if i >= 2:
            for copy in copies[i - 2]:
                copy.wait()
        copies.append([])
        for f in range(many):
            if by_row:
                held[i % 2, f] = out[:, f * hid : (f + 1) * hid].astype(BF16)
                target = outs[f].at[there, :]
            else:
                held[i % 2, f] = out.astype(BF16)
                target = outs[f].at[:, there]
            copies[i].append(pltpu.make_async_copy(held.at[i % 2, f], target, sems.at[i % 2, f]))
            copies[i][f].start()
    for group in copies[-2:]:
        for copy in group:
            copy.wait()


def weight_gradients(core, owns, others, factors, by_row):
    n = len(owns)
    many = len(factors)
    rows, hid = factors[0][0].shape
    half = (owns[0].shape[1] - LANES) // 2
    step = half // 2
    width = 2 * half
    tile = (step, hid) if by_row else (hid, step)
    return pl.pallas_call(
        functools.partial(weights_kernel, n, many, by_row, step),
        out_shape=[jax.ShapeDtypeStruct((width, hid) if by_row else (hid, width), BF16)] * many,
        in_specs=[SMEM] + [VMEM] * (2 * n + many * n),
        out_specs=[ANY] * many,
        scratch_shapes=[
            pltpu.VMEM((n * rows, many * hid) if by_row else (hid, n * rows), BF16),
            pltpu.VMEM((2, many) + tile, BF16),
            pltpu.SemaphoreType.DMA((2, many)),
        ],
        compiler_params=params(24),
        cost_estimate=cost(rows * width * hid, 2 * n * rows * width),
    )(core, *owns, *others, *(a for f in factors for a in f))


def place_kernel(core_ref, own_ref, other_ref, out_hbm, sems):
    half = out_hbm.shape[1] // 2
    copies = []
    for i, (ref, c) in enumerate(((own_ref, core_ref[0]), (other_ref, 1 - core_ref[0]))):
        there = pl.ds(pl.multiple_of(c * half, LANES), half)
        copies.append(pltpu.make_async_copy(ref.at[:, pl.ds(0, half)], out_hbm.at[:, there], sems.at[i]))
    for copy in copies:
        copy.start()
    for copy in copies:
        copy.wait()


def place_halves(core, own, other, width):
    return pl.pallas_call(
        place_kernel,
        out_shape=jax.ShapeDtypeStruct((own.shape[0], width), BF16),
        in_specs=[SMEM, VMEM, VMEM],
        out_specs=ANY,
        scratch_shapes=[pltpu.SemaphoreType.DMA((2,))],
        compiler_params=params(8),
        cost_estimate=cost(1, 4 * own.shape[0] * width),
    )(core, own, other)


def on_device(tokens, grad_out, routes, probs, w_gate, w_up, w_down):
    experts = lax.axis_size("expert")
    tok, width = tokens.shape
    top = routes.shape[1]
    cap = 3 * tok * top // experts
    plane = experts // RINGS
    half = width // 2
    me = lax.axis_index("expert")
    core_id = lax.axis_index("tensor")
    core = core_id.astype(jnp.int32).reshape(1)
    z, p = me // plane, me % plane
    weights = (w_gate[0], w_up[0], w_down[0])

    after = {0: 1, 1: 3, 3: 2, 2: 0}
    ring = [(i, after[i // plane] * plane + i % plane) for i in range(experts)]
    peers = [[(i, i // plane * plane + ((i % plane) ^ j)) for i in range(experts)] for j in range(plane)]
    swap = [(0, 1), (1, 0)]

    row = jnp.arange(plane * cap, dtype=jnp.int32)
    codes = (z * plane + (p ^ (row // cap))) * cap + row % cap
    codes = jnp.broadcast_to(codes.astype(F32)[:, None], (plane * cap, LANES))
    meet = lax.optimization_barrier

    def hop(rows):
        return lax.ppermute(rows, "expert", ring)

    def turn(rows):
        return lax.ppermute(rows, "tensor", swap)

    def exchange(parts):
        return [parts[0]] + [lax.ppermute(parts[j], "expert", peers[j]) for j in range(1, plane)]

    def joined(parts):
        return jnp.concatenate(parts, axis=0)

    def work(own, other):
        mine, send, *kept = expert_rows(core, own, other, *weights)
        return mine, send, kept

    def summed(mine, came):
        total = (mine + came.astype(F32)).astype(BF16)
        return [total[j * cap : (j + 1) * cap] for j in range(plane)]

    def picked(block, *waits):
        return list(choose(codes, block, waits, tok, top, cap))

    def gather(block, parts, came=None, waits=(), flat=True):
        return gather_tokens(codes, block, parts, came, waits, top, cap, flat)

    h0 = make_block(core, tokens, grad_out, routes, probs)

    h1 = hop(h0)
    g0 = exchange(picked(h0))
    h1, g0, mark = meet((h1, g0, follow(h1, *g0)))

    h2 = hop(h1)
    g1 = exchange(picked(h1, mark))
    own0 = joined(g0)
    other0 = turn(own0)
    mine0, send0, w0 = work(own0, other0)
    came0 = turn(send0)
    h2, g1, mine0, came0, w0, mark = meet((h2, g1, mine0, came0, w0, follow(h2, *g1)))

    h3 = hop(h2)
    g2 = exchange(picked(h2, mark))
    own1 = joined(g1)
    other1 = turn(own1)
    mine1, send1, w1 = work(own1, other1)
    s3 = picked(h3, *g2, send1)
    h3, s3, g2, mine1, send1, w1 = meet((h3, s3, g2, mine1, send1, w1))

    g3 = exchange(s3)
    b1 = exchange(summed(mine1, turn(send1)))
    own2 = joined(g2)
    other2 = turn(own2)
    mine2, send2, w2 = work(own2, other2)
    t1 = gather(h1, b1, waits=(*g3, send2))
    g3, t1, mine2, send2, w2, mine0 = meet((g3, t1, mine2, send2, w2, mine0))

    r1 = hop(t1)
    b2 = exchange(summed(mine2, turn(send2)))
    own3 = joined(g3)
    other3 = turn(own3)
    mine3, send3, w3 = work(own3, other3)
    came3 = turn(send3)
    t2 = gather(h2, b2, r1)
    t2, mine3, came3, w3, mine0 = meet((t2, mine3, came3, w3, mine0))

    owns, others = (own0, own1, own2, own3), (other0, other1, other2, other3)
    ph, gg, gu = zip(w0, w1, w2, w3)
    r2 = hop(t2)
    b3 = exchange(summed(mine3, came3))
    d_gate, d_up = weight_gradients(core, owns, others, (gg, gu), True)
    c0 = summed(mine0, came0)
    t3 = gather(h3, b3, r2)
    t3, d_gate, d_up, ph, c0 = meet((t3, d_gate, d_up, ph, c0))

    r3 = hop(t3)
    b0 = exchange(c0)
    (d_down,) = weight_gradients(core, owns, others, (ph,), False)
    r3, b0, d_down = meet((r3, b0, d_down))
    total, dp = gather(h0, b0, r3, flat=False)

    d_tokens = place_halves(core, total, turn(total), width)
    d_probs = dp[:top, :].T
    return (d_tokens, d_probs, d_gate[None], d_up[None], d_down[None])


def solution(mesh):
    rows = P("expert", None)
    columns = P("expert", None, "tensor")
    down = P("expert", "tensor", None)
    return jax.shard_map(
        on_device,
        mesh=mesh,
        in_specs=(rows, rows, rows, rows, columns, columns, down),
        out_specs=(rows, rows, columns, columns, down),
        check_vma=False,
    )
```

```python
import functools

import jax
import jax.numpy as jnp
from jax import lax
from jax.experimental import pallas as pl
from jax.experimental.pallas import tpu as pltpu
from jax.sharding import PartitionSpec as P

BF16 = jnp.bfloat16
F32 = jnp.float32
LANES = 128
FIELDS = 16
RINGS = 4
VMEM = pl.BlockSpec(memory_space=pltpu.VMEM)
SMEM = pl.BlockSpec(memory_space=pltpu.SMEM)
ANY = pl.BlockSpec(memory_space=pl.ANY)


def dot(a, b, dims):
    return lax.dot_general(a, b, (dims, ((), ())), preferred_element_type=F32)


def params(mib):
    return pltpu.CompilerParams(vmem_limit_bytes=mib * 2**20)


def cost(flops, nbytes):
    return pl.CostEstimate(flops=flops, bytes_accessed=nbytes, transcendentals=0)


CLAIM = 4 * 10**10


def tiles(ref, tok):
    return jnp.concatenate([ref[i * tok : (i + 1) * tok, :] for i in range(ref.shape[0] // tok)], axis=1)


def put_tiles(ref, value):
    tok = value.shape[0]
    for i in range(value.shape[1] // LANES):
        ref[i * tok : (i + 1) * tok, :] = value[:, i * LANES : (i + 1) * LANES]


def block_kernel(tok_ref, dy_ref, routes_ref, probs_ref, out_ref):
    top, tok = routes_ref.shape
    tall = tok_ref.shape[1] * tok // LANES
    expert = lax.broadcasted_iota(jnp.int32, (LANES, tok), 0)
    row = lax.broadcasted_iota(jnp.int32, (tok, tok), 0)
    col = lax.broadcasted_iota(jnp.int32, (tok, tok), 1)
    hot = [expert == routes_ref[k : k + 1, :] for k in range(top)]
    named = sum(jnp.where(h, 1.0, 0.0) for h in hot).astype(BF16)
    before = jnp.where(row < col, 1.0, 0.0).astype(BF16)
    counts = dot(named, before, ((1,), (0,)))
    field = lax.broadcasted_iota(jnp.int32, (FIELDS, LANES), 0)
    aux = jnp.zeros((FIELDS, LANES), F32)
    for k in range(top):
        slot = jnp.sum(jnp.where(hot[k], counts, 0.0), axis=0, keepdims=True)
        aux = jnp.where(field == k, routes_ref[k : k + 1, :].astype(F32), aux)
        aux = jnp.where(field == top + k, slot, aux)
        aux = jnp.where(field == 2 * top + k, probs_ref[k : k + 1, :].astype(F32), aux)
    for i, ref in enumerate((tok_ref, dy_ref)):
        put_tiles(out_ref.at[pl.ds(i * tall, tall), :], ref[...])
    out_ref[2 * tall :, :] = aux.astype(BF16)


def make_block(core, tokens, grad_out, routes, probs):
    tok, width = tokens.shape
    half = width // 2
    mine = [lax.dynamic_slice_in_dim(a, core[0] * half, half, axis=1) for a in (tokens, grad_out)]
    return pl.pallas_call(
        block_kernel,
        out_shape=jax.ShapeDtypeStruct((tok * width // LANES + FIELDS, LANES), BF16),
        in_specs=[VMEM] * 4,
        out_specs=VMEM,
        compiler_params=params(8),
        cost_estimate=cost(2 * tok * tok * LANES, 4 * tok * width),
    )(*mine, routes.T, probs.T)


def follow_kernel(*refs):
    refs[-1][...] = jnp.zeros_like(refs[-1])


def follow(*arrays):
    return pl.pallas_call(
        follow_kernel,
        out_shape=jax.ShapeDtypeStruct((8, LANES), F32),
        in_specs=[ANY] * len(arrays),
        out_specs=VMEM,
        compiler_params=params(4),
        cost_estimate=cost(CLAIM, 1),
    )(*arrays)


def hits(top, cap, aux, codes):
    aux = aux.astype(F32)
    return [codes == aux[k : k + 1] * cap + aux[top + k : top + k + 1] for k in range(top)], aux


def choose_kernel(top, cap, waits, codes_ref, block_ref, *refs):
    outs = refs[waits:]
    tall = block_ref.shape[0] - FIELDS
    body = outs[0].shape[1] - LANES
    hit, aux = hits(top, cap, block_ref[tall:, :], codes_ref[...])
    both = sum(jnp.where(h, 1.0, 0.0) for h in hit).astype(BF16)
    rows = dot(both, tiles(block_ref.at[pl.ds(0, tall), :], tall * LANES // body), ((1,), (0,))).astype(BF16)
    prob = sum(jnp.where(hit[k], aux[2 * top + k : 2 * top + k + 1], 0.0) for k in range(top))
    prob = jnp.broadcast_to(jnp.sum(prob, axis=1, keepdims=True), (rows.shape[0], LANES)).astype(BF16)
    for j, out in enumerate(outs):
        out[:, :body] = rows[j * cap : (j + 1) * cap]
        out[:, body:] = prob[j * cap : (j + 1) * cap]


def choose(codes, block, waits, tok, top, cap):
    rows = codes.shape[0]
    wide = (block.shape[0] - FIELDS) * LANES // tok + LANES
    return pl.pallas_call(
        functools.partial(choose_kernel, top, cap, len(waits)),
        out_shape=[jax.ShapeDtypeStruct((cap, wide), BF16)] * (rows // cap),
        in_specs=[VMEM, VMEM] + [ANY] * len(waits),
        out_specs=[VMEM] * (rows // cap),
        compiler_params=params(12),
        cost_estimate=cost(CLAIM if len(waits) > 1 else 1, 2 * wide * (rows + tok)),
    )(codes, block, *waits)


def expert_kernel(core_ref, own_ref, other_ref, wg, wu, wd, mine_ref, send_ref, ph_ref, gg_ref, gu_ref):
    half = own_ref.shape[1] // 2 // LANES * LANES
    sides = [pl.ds(pl.multiple_of(c * half, LANES), half) for c in (core_ref[0], 1 - core_ref[0])]
    gate = up = raw = 0.0
    for ref, side in zip((own_ref, other_ref), sides):
        x, dy = ref[:, :half], ref[:, half : 2 * half]
        gate = gate + dot(x, wg[side, :], ((1,), (0,)))
        up = up + dot(x, wu[side, :], ((1,), (0,)))
        raw = raw + dot(dy, wd[:, side], ((1,), (1,)))
    prob = own_ref[:, 2 * half :].astype(F32)[:, :1]
    sigma = jax.nn.sigmoid(gate)
    act = gate * sigma
    hidden = (act * up).astype(BF16).astype(F32)
    row_part = jnp.sum(hidden * raw, axis=1, keepdims=True)
    grad_h = prob * raw
    g_up = (grad_h * act).astype(BF16)
    g_gate = (grad_h * up * sigma * (1.0 + gate * (1.0 - sigma))).astype(BF16)
    ph_ref[...] = (prob * hidden).astype(BF16)
    gg_ref[...] = g_gate
    gu_ref[...] = g_up
    row_part = jnp.broadcast_to(row_part, (row_part.shape[0], LANES))
    mine_ref[:, half:] = row_part.astype(BF16).astype(F32)
    send_ref[:, half:] = row_part.astype(BF16)
    for ref, side in zip((mine_ref, send_ref), sides):
        part = dot(g_gate, wg[side, :], ((1,), (1,))) + dot(g_up, wu[side, :], ((1,), (1,)))
        ref[:, :half] = part.astype(ref.dtype)


def expert_rows(core, own, other, gate_w, up_w, down_w):
    rows = own.shape[0]
    width, hid = gate_w.shape
    half = width // 2
    shape = jax.ShapeDtypeStruct
    return pl.pallas_call(
        expert_kernel,
        out_shape=[shape((rows, half + LANES), F32), shape((rows, half + LANES), BF16)] + [shape((rows, hid), BF16)] * 3,
        in_specs=[SMEM] + [VMEM] * 5,
        out_specs=[VMEM] * 5,
        compiler_params=params(16),
        cost_estimate=cost(10 * rows * width * hid, 4 * rows * width),
    )(core, own, other, gate_w, up_w, down_w)


def gather_kernel(top, cap, n, adds, flat, codes_ref, aux_ref, *refs):
    parts, out = refs[:n], refs[-1]
    half = parts[0].shape[1] - LANES
    hit, _ = hits(top, cap, aux_ref[...], codes_ref[...])
    tok = codes_ref.shape[1]
    rows = jnp.concatenate([r[...] for r in parts], axis=0)
    both = sum(jnp.where(h, 1.0, 0.0) for h in hit).astype(BF16)
    sums = dot(both, rows[:, :half], ((0,), (0,)))
    row_dp = rows[:, half:].astype(F32)
    field = lax.broadcasted_iota(jnp.int32, (FIELDS, LANES), 0)
    dp = jnp.zeros((FIELDS, LANES), F32)
    for k in range(top):
        dp = jnp.where(field == k, jnp.sum(jnp.where(hit[k], row_dp, 0.0), axis=0, keepdims=True), dp)
    tall = tok * half // LANES
    if adds:
        sums = sums + tiles(refs[n].at[pl.ds(0, tall), :], tok).astype(F32)
        dp = dp + refs[n][tall:, :].astype(F32)
    if flat:
        put_tiles(out, sums.astype(BF16))
        out[tall:, :] = dp.astype(BF16)
    else:
        refs[-2][...] = sums.astype(BF16)
        out[...] = dp.astype(BF16)


def gather_tokens(codes, block, parts, came, waits, top, cap, flat):
    tok = codes.shape[1]
    half = parts[0].shape[1] - LANES
    n = len(parts)
    extra = [] if came is None else [came]
    waits = list(waits)
    whole = lambda a: pl.BlockSpec(a.shape, lambda i: (0, 0))
    tail = pl.BlockSpec((FIELDS, LANES), lambda i: (block.shape[0] // FIELDS - 1, 0))
    out = jax.ShapeDtypeStruct((tok * half // LANES + FIELDS, LANES), BF16)
    if not flat:
        out = [jax.ShapeDtypeStruct((tok, half), BF16), jax.ShapeDtypeStruct((FIELDS, LANES), BF16)]
    return pl.pallas_call(
        functools.partial(gather_kernel, top, cap, n, came is not None, flat),
        out_shape=out,
        grid=(1,),
        in_specs=[whole(codes), tail] + [whole(a) for a in parts + extra] + [ANY] * len(waits),
        out_specs=jax.tree.map(whole, out),
        compiler_params=params(12),
        cost_estimate=cost(CLAIM, 6 * tok * half),
    )(codes, block, *parts, *extra, *waits)


def weights_kernel(n, many, by_row, step, core_ref, *refs):
    sides = refs[:n], refs[n : 2 * n]
    factors = refs[2 * n : 2 * n + many * n]
    outs, (fixed, held, sems) = refs[2 * n + many * n : -3], refs[-3:]
    rows, hid = factors[0].shape
    half = sides[0][0].shape[1] // 2 // LANES * LANES
    parts = half // step
    first = 0 if by_row else half
    for f in range(many):
        for k in range(n):
            part = factors[f * n + k][...]
            if by_row:
                fixed[k * rows : (k + 1) * rows, f * hid : (f + 1) * hid] = part
            else:
                fixed[:, k * rows : (k + 1) * rows] = part.astype(F32).T.astype(BF16)
    copies = []
    for i in range(2 * parts):
        side, at = i // parts, first + i % parts * step
        data = jnp.concatenate([r[:, at : at + step] for r in sides[side]], axis=0)
        out = dot(data, fixed[...], ((0,), (0,))) if by_row else dot(fixed[...], data, ((1,), (0,)))
        c = core_ref[0] if side == 0 else 1 - core_ref[0]
        there = pl.ds(pl.multiple_of(c * half + i % parts * step, LANES), step)
        if i >= 2:
            for copy in copies[i - 2]:
                copy.wait()
        copies.append([])
        for f in range(many):
            if by_row:
                held[i % 2, f] = out[:, f * hid : (f + 1) * hid].astype(BF16)
                target = outs[f].at[there, :]
            else:
                held[i % 2, f] = out.astype(BF16)
                target = outs[f].at[:, there]
            copies[i].append(pltpu.make_async_copy(held.at[i % 2, f], target, sems.at[i % 2, f]))
            copies[i][f].start()
    for group in copies[-2:]:
        for copy in group:
            copy.wait()


def weight_gradients(core, owns, others, factors, by_row):
    n = len(owns)
    many = len(factors)
    rows, hid = factors[0][0].shape
    half = (owns[0].shape[1] - LANES) // 2
    step = half // 2
    width = 2 * half
    tile = (step, hid) if by_row else (hid, step)
    return pl.pallas_call(
        functools.partial(weights_kernel, n, many, by_row, step),
        out_shape=[jax.ShapeDtypeStruct((width, hid) if by_row else (hid, width), BF16)] * many,
        in_specs=[SMEM] + [VMEM] * (2 * n + many * n),
        out_specs=[ANY] * many,
        scratch_shapes=[
            pltpu.VMEM((n * rows, many * hid) if by_row else (hid, n * rows), BF16),
            pltpu.VMEM((2, many) + tile, BF16),
            pltpu.SemaphoreType.DMA((2, many)),
        ],
        compiler_params=params(24),
        cost_estimate=cost(rows * width * hid, 2 * n * rows * width),
    )(core, *owns, *others, *(a for f in factors for a in f))


def place_kernel(core_ref, own_ref, other_ref, out_hbm, sems):
    half = out_hbm.shape[1] // 2
    copies = []
    for i, (ref, c) in enumerate(((own_ref, core_ref[0]), (other_ref, 1 - core_ref[0]))):
        there = pl.ds(pl.multiple_of(c * half, LANES), half)
        copies.append(pltpu.make_async_copy(ref.at[:, pl.ds(0, half)], out_hbm.at[:, there], sems.at[i]))
    for copy in copies:
        copy.start()
    for copy in copies:
        copy.wait()


def place_halves(core, own, other, width):
    return pl.pallas_call(
        place_kernel,
        out_shape=jax.ShapeDtypeStruct((own.shape[0], width), BF16),
        in_specs=[SMEM, VMEM, VMEM],
        out_specs=ANY,
        scratch_shapes=[pltpu.SemaphoreType.DMA((2,))],
        compiler_params=params(8),
        cost_estimate=cost(1, 4 * own.shape[0] * width),
    )(core, own, other)


def on_device(tokens, grad_out, routes, probs, w_gate, w_up, w_down):
    experts = lax.axis_size("expert")
    tok, width = tokens.shape
    top = routes.shape[1]
    cap = 3 * tok * top // experts
    plane = experts // RINGS
    half = width // 2
    me = lax.axis_index("expert")
    core_id = lax.axis_index("tensor")
    core = core_id.astype(jnp.int32).reshape(1)
    z, p = me // plane, me % plane
    weights = (w_gate[0], w_up[0], w_down[0])

    after = {0: 1, 1: 3, 3: 2, 2: 0}
    ring = [(i, after[i // plane] * plane + i % plane) for i in range(experts)]
    peers = [[(i, i // plane * plane + ((i % plane) ^ j)) for i in range(experts)] for j in range(plane)]
    swap = [(0, 1), (1, 0)]

    row = jnp.arange(plane * cap, dtype=jnp.int32)
    codes = (z * plane + (p ^ (row // cap))) * cap + row % cap
    codes = jnp.broadcast_to(codes.astype(F32)[:, None], (plane * cap, LANES))
    meet = lax.optimization_barrier

    def hop(rows):
        return lax.ppermute(rows, "expert", ring)

    def turn(rows):
        return lax.ppermute(rows, "tensor", swap)

    def exchange(parts):
        return [parts[0]] + [lax.ppermute(parts[j], "expert", peers[j]) for j in range(1, plane)]

    def joined(parts):
        return jnp.concatenate(parts, axis=0)

    def work(own, other):
        mine, send, *kept = expert_rows(core, own, other, *weights)
        return mine, send, kept

    def summed(mine, came):
        total = (mine + came.astype(F32)).astype(BF16)
        return [total[j * cap : (j + 1) * cap] for j in range(plane)]

    def picked(block, *waits):
        return list(choose(codes, block, waits, tok, top, cap))

    def gather(block, parts, came=None, waits=(), flat=True):
        return gather_tokens(codes, block, parts, came, waits, top, cap, flat)

    h0 = make_block(core, tokens, grad_out, routes, probs)

    h1 = hop(h0)
    g0 = exchange(picked(h0))
    h1, g0, mark = meet((h1, g0, follow(h1, *g0)))

    h2 = hop(h1)
    g1 = exchange(picked(h1, mark))
    own0 = joined(g0)
    other0 = turn(own0)
    mine0, send0, w0 = work(own0, other0)
    h2, g1, mine0, send0, w0, mark = meet((h2, g1, mine0, send0, w0, follow(h2, *g1, send0)))

    h3 = hop(h2)
    g2 = exchange(picked(h2, mark))
    own1 = joined(g1)
    other1 = turn(own1)
    mine1, send1, w1 = work(own1, other1)
    came0 = turn(send0)
    s3 = picked(h3, *g2, send1)
    h3, s3, g2, came0, mine1, send1, w1 = meet((h3, s3, g2, came0, mine1, send1, w1))

    g3 = exchange(s3)
    b1 = exchange(summed(mine1, turn(send1)))
    own2 = joined(g2)
    other2 = turn(own2)
    mine2, send2, w2 = work(own2, other2)
    t1 = gather(h1, b1, waits=(*g3, send2))
    g3, t1, mine2, send2, w2, mine0 = meet((g3, t1, mine2, send2, w2, mine0))

    r1 = hop(t1)
    b2 = exchange(summed(mine2, turn(send2)))
    own3 = joined(g3)
    other3 = turn(own3)
    mine3, send3, w3 = work(own3, other3)
    came3 = turn(send3)
    t2 = gather(h2, b2, r1)
    t2, mine3, came3, w3, mine0 = meet((t2, mine3, came3, w3, mine0))

    owns, others = (own0, own1, own2, own3), (other0, other1, other2, other3)
    ph, gg, gu = zip(w0, w1, w2, w3)
    r2 = hop(t2)
    b3 = exchange(summed(mine3, came3))
    d_gate, d_up = weight_gradients(core, owns, others, (gg, gu), True)
    c0 = summed(mine0, came0)
    t3 = gather(h3, b3, r2)
    t3, d_gate, d_up, ph, c0 = meet((t3, d_gate, d_up, ph, c0))

    r3 = hop(t3)
    b0 = exchange(c0)
    (d_down,) = weight_gradients(core, owns, others, (ph,), False)
    r3, b0, d_down = meet((r3, b0, d_down))
    total, dp = gather(h0, b0, r3, flat=False)

    d_tokens = place_halves(core, total, turn(total), width)
    d_probs = dp[:top, :].T
    return (d_tokens, d_probs, d_gate[None], d_up[None], d_down[None])


def solution(mesh):
    rows = P("expert", None)
    columns = P("expert", None, "tensor")
    down = P("expert", "tensor", None)
    return jax.shard_map(
        on_device,
        mesh=mesh,
        in_specs=(rows, rows, rows, rows, columns, columns, down),
        out_specs=(rows, rows, columns, columns, down),
        check_vma=False,
    )
```
